512 devices in a mesh: bank: 64 (over z, y_lo, core), dp: 8 (over y_hi, x).
Axes of the slice: x: 4, y: 8 (y_hi: 2, y_lo: 4; y = y_hi * 4 + y_lo), z: 8, core: 2. Of those that a mesh axis runs over, the one named last changes fastest.
Arguments:
- queries: bfloat16 [131072, 1024], P(('bank', 'dp')), may hold values from -6 to 6
- w_input: bfloat16 [1024, 1024], P('dp'), may hold values from -0.1875 to 0.1875
- w_output: bfloat16 [1024, 256], P('dp'), may hold values from -0.1875 to 0.1875
- item_bank: bfloat16 [8192, 256], P('bank'), may hold values from -6 to 6
- positives: int32 [131072], P(('bank', 'dp')), may hold values from 0 to 8191
- fresh_rows: bfloat16 [4096, 256], P('bank'), may hold values from -6 to 6
- owners: int32 [4096, 1], P('bank'), may hold values from 0 to 63; in each aligned block of 64 rows (0 to 63, 64 to 127, ...) at most 2 rows name the same one
- slots: int32 [4096], P('bank'), may hold values from 0 to 127
Outputs:
- contrast_loss: float32 [131072], P(('bank', 'dp'))
- next_bank: bfloat16 [8192, 256], P('bank')
The draws below stay inside these ranges and needn't reach their ends.
Inputs may be any that keep to these rules, and one draw needn't show every extreme that they name: `owners`: among the 64 rows of one index of bank, at most 2 name the same owner; some owner is named by exactly 2 of them.
All inputs are finite; a program needn't handle non-finite values.
Results may differ from the reference program's by a relative error of at most 0.0022.
Values may be sent and summed in bfloat16 or wider, within the bound.
No kernel may reach another device: no remote copies, remote signals or barrier semaphores. Data moves between devices by JAX's collectives and lax.ppermute only.
A program may use at most 64 MiB of HBM per device.

```python
import math
import jax
import jax.numpy as jnp
import numpy as np
from jax import lax

D = 1024
HID = 1024
E = 256
Q_DEV = 256
BANK_DEV = 128
F_DEV = 64
QUERIES = 131072
BANK = 8192
FRESH = 4096
CAP = 2
N_BANK = 64


def draw_item_bank(key, part):
    key = jax.random.fold_in(key, 11)
    first_key = jax.random.fold_in(key, 0)
    values = jnp.clip(0.25 * jax.random.normal(first_key, (BANK, E), jnp.float32), -1.5, 1.5)
    return values.astype(jnp.bfloat16)


def set_ends(array, own_key, least, top_value):
    shape = array.shape
    place = [jax.random.randint(jax.random.fold_in(own_key, axis), (), 0, shape[axis]) for axis in range(len(shape))]
    array = array.at[tuple(place)].set(least)
    longest = shape.index(max(shape))
    place[longest] = (place[longest] + 1) % shape[longest]
    return array.at[tuple(place)].set(top_value)


def block_scale(stream_key, dims, shards, low, largest):
    level, own = 1.0, jax.random.fold_in(stream_key, 6)
    for axis_at, shards_of in shards:
        draws = jnp.exp(jax.random.uniform(jax.random.fold_in(own, axis_at), (shards_of,), jnp.float32, low / len(shards), largest / len(shards)))
        level = level * jnp.repeat(draws, dims[axis_at] // shards_of).reshape([-1 if axis == axis_at else 1 for axis in range(len(dims))])
    return level


def deal_out(key, own, number, rows, number_of, top, most, lean):
    ranking = jax.random.permutation(key, number_of)
    packed, ordinary = load_shares(number_of, rows * top, most, lean, True), load_shares(number_of, rows * top, most, lean, False)
    places = jnp.arange(number_of)

    def named(sizes, turn):
        used = int((sizes > 0).sum())
        fixed = max(1, used // 4)
        shifted = fixed + (places - fixed + turn * (used - fixed)) % max(1, number_of - fixed)
        return jnp.zeros((number_of,), jnp.int32).at[ranking[jnp.where(places < fixed, places, shifted)]].set(jnp.asarray(sizes, jnp.int32))

    sizes = jnp.where(number % 4 == 0, named(packed, number // 4), named(ordinary, number - number // 4 - 1))
    mixed = jax.random.permutation(jax.random.fold_in(own, 3), number_of)
    source_of, taker = mixed[0:number_of // 2 * 2:2], mixed[1:number_of // 2 * 2:2]
    margin = jnp.minimum(sizes[source_of] - 1, most - sizes[taker]) // 2
    margin = jnp.where((source_of == ranking[0]) | (taker == ranking[0]) | (sizes[taker] == 0), 0, jnp.maximum(margin, 0))
    shifted = jax.random.randint(jax.random.fold_in(own, 4), (number_of // 2,), 0, 1 << 20) % (margin + 1)
    sizes = sizes.at[source_of].add(-shifted).at[taker].add(shifted)
    labels = jnp.searchsorted(jnp.cumsum(sizes), jnp.arange(rows * top), side="right").astype(jnp.int32)
    table = labels.reshape(top, rows).T
    table = table[jax.random.permutation(jax.random.fold_in(own, 1), rows)]
    turn = jax.random.randint(jax.random.fold_in(own, 2), (rows, 1), 0, top)
    return jnp.take_along_axis(table, (jnp.arange(top)[None, :] + turn) % top, axis=1)


def load_shares(number_of, total, reach, lean, full):
    loads = [(1 << 20) // math.isqrt(grade ** lean) + 1 for grade in range(1, number_of + 1)]
    largest = reach if full else min(reach, max(-(-total // number_of), total * loads[0] // sum(loads)))
    least = 1 if total - largest >= number_of - 1 else 0
    given, rest = [largest] + [least] * (number_of - 1), total - largest - least * (number_of - 1)
    while rest > 0:
        candidates = [i for i in range(1, number_of) if given[i] < largest] or [i for i in range(1, number_of) if given[i] < reach]
        whole, remaining = sum([loads[i] for i in candidates]), rest
        for i in candidates:
            extra = min(reach - given[i], max(1, remaining * loads[i] // whole), rest)
            given[i] = given[i] + extra
            rest = rest - extra
    return np.array(given)


def scatter_about(rng, shape, scale, bound, shards=(), kind=jnp.bfloat16):
    level = block_scale(rng, shape, shards, -0.22, 0.18) if shards else 1.0
    values = jax.random.normal(rng, shape, jnp.float32) * scale * level
    return jnp.minimum(jnp.maximum(values, -bound), bound).astype(kind)


def setup_inputs(seed: int = 0) -> dict:
    keys = jax.random.split(jax.random.key(seed), 9)
    queries = scatter_about(keys[0], (QUERIES, D), 1.0, 6.0, ((0, 512),))
    w_input = scatter_about(keys[1], (D, HID), D ** -0.5, 0.1875, ((0, 8),))
    w_output = scatter_about(keys[2], (HID, E), HID ** -0.5, 0.1875, ((0, 8),))
    item_bank = draw_item_bank(jax.random.fold_in(keys[8], 71), 0)
    positives = set_ends(jax.random.randint(keys[4], (QUERIES,), 0, BANK), jax.random.fold_in(keys[4], 1), 0, BANK - 1).astype(jnp.int32)
    fresh_rows = scatter_about(keys[5], (FRESH, E), 1.0, 6.0, ((0, 64),))
    owners_keys = jax.random.split(jax.random.fold_in(keys[6], 1), FRESH // F_DEV)
    owners_turns = jax.random.permutation(jax.random.fold_in(keys[6], 3), FRESH // F_DEV)
    owners = jax.vmap(lambda own, number: deal_out(jax.random.fold_in(keys[6], 2), own, number, F_DEV, N_BANK, 1, CAP, 1))(owners_keys, owners_turns).reshape((FRESH, 1))
    slots = set_ends(jax.random.randint(keys[7], (FRESH,), 0, BANK_DEV), jax.random.fold_in(keys[7], 1), 0, BANK_DEV - 1).astype(jnp.int32)
    return dict(queries=queries, w_input=w_input, w_output=w_output, item_bank=item_bank, positives=positives, fresh_rows=fresh_rows, owners=owners, slots=slots)


def reference(queries, w_input, w_output, item_bank, positives, fresh_rows, owners, slots):
    preact = jnp.dot(queries, w_input, preferred_element_type=jnp.float32)
    hidden = jax.nn.silu(preact).astype(jnp.bfloat16)
    embedding = jnp.dot(hidden, w_output, preferred_element_type=jnp.float32)
    unit_query = (embedding * lax.rsqrt(lax.optimization_barrier(jnp.sum(embedding * embedding, axis=1, keepdims=True)) + 1e-06)).astype(jnp.bfloat16)
    blocks = unit_query.reshape(QUERIES // Q_DEV, Q_DEV, E)
    targets = positives.reshape(QUERIES // Q_DEV, Q_DEV)

    def score_block(inputs):
        block_query, block_target = inputs
        logits = 16.0 * jnp.dot(block_query, item_bank.T, preferred_element_type=jnp.float32)
        spread = jax.nn.logsumexp(logits, axis=1)
        picked = jnp.take_along_axis(logits, block_target[:, None].astype(jnp.int32), axis=1)[:, 0]
        return spread - picked
    contrast_loss = lax.map(score_block, (blocks, targets)).reshape(QUERIES)
    target_rows = (owners[:, 0] * BANK_DEV + slots).astype(jnp.int32)
    winner = jnp.full((BANK,), -1, jnp.int32).at[target_rows].max(jnp.arange(FRESH, dtype=jnp.int32))
    chosen = fresh_rows[jnp.maximum(winner, 0)]
    next_bank = jnp.where(winner[:, None] >= 0, chosen, item_bank)
    return (contrast_loss, next_bank)
```

```python
import functools
import math

import jax
import jax.numpy as jnp
from jax import lax
from jax.experimental import pallas as pl
from jax.experimental.pallas import tpu as pltpu
from jax.sharding import PartitionSpec as P

BF16 = jnp.bfloat16
F32 = jnp.float32
I32 = jnp.int32

CORES = 2
X = 4

VMEM = pltpu.VMEM
LIMIT = 48 * 1024 * 1024


def core_index():
    return lax.rem(lax.axis_index("bank"), CORES)


def x_index():
    return lax.rem(lax.axis_index("dp"), X)


def call(kernel, outs, args, scratch=()):
    return pl.pallas_call(
        kernel,
        out_shape=outs,
        in_specs=[pl.BlockSpec(memory_space=VMEM)] * len(args),
        out_specs=jax.tree.map(lambda _: pl.BlockSpec(memory_space=VMEM), outs),
        scratch_shapes=list(scratch),
        compiler_params=pltpu.CompilerParams(vmem_limit_bytes=LIMIT),
    )(*args)


def weights_kernel(w_input, w_output, out):
    half = w_input.shape[1] // CORES
    out_half = w_output.shape[1] // CORES
    rows = w_input.shape[0]
    core = core_index()
    first = w_input[:, pl.ds(pl.multiple_of(core * half, half), half)]
    second = w_output[:, pl.ds(pl.multiple_of(core * out_half, out_half), out_half)]
    pieces = half // out_half
    tall = rows // pieces
    for d in range(out.shape[0]):
        out[d, :rows, :] = first
        for i in range(pieces):
            out[d, rows:, i * out_half : (i + 1) * out_half] = second[i * tall : (i + 1) * tall, :]


def outbox_kernel(owners, slots, fresh, bank, out):
    part = bank.shape[0] // X
    x = x_index()
    own = bank[pl.ds(pl.multiple_of(x * part, part), part), :]
    chips = out.shape[0]
    for k in range(chips):
        out[k, :part, :] = own
    count = fresh.shape[0]
    owner = owners[...].astype(F32)
    across = jnp.broadcast_to(owner, (count, count))
    earlier = lax.broadcasted_iota(I32, (count, count), 0) < lax.broadcasted_iota(I32, (count, count), 1)
    same = across == across.T
    placed = jnp.sum(jnp.where(same & earlier, 1.0, 0.0), axis=0, keepdims=True)
    key = (owner * 2.0 + placed).astype(I32)
    row = lax.broadcasted_iota(I32, (chips * 8, count), 0)
    wanted = (row // 8) * 4 + (row % 4)
    chosen = wanted == key
    data = jnp.dot(chosen.astype(BF16), fresh[...], preferred_element_type=F32)
    slot = jnp.sum(jnp.where(chosen, slots[...].astype(F32) + 1.0, 0.0), axis=1, keepdims=True) - 1.0
    kind = lax.broadcasted_iota(I32, data.shape, 0) % 8
    both = jnp.where(kind < 4, data, slot).astype(BF16)
    out[:, part:, :] = both.reshape(chips, 8, both.shape[1])


def tower_kernel(queries, w_own, w_other, positives, out, hidden, w_last, unit):
    core = core_index()
    members, tall, half = w_own.shape
    rows = queries.shape[1] // members
    out_half = w_last.shape[1] // CORES
    pieces = half // out_half
    step = tall - rows
    q = queries[...]
    for which, w in ((core, w_own), (1 - core, w_other)):
        first = w[:, :rows, :].reshape(members * rows, half)
        v = jnp.dot(q, first, preferred_element_type=F32)
        v = (0.5 * v) * (1.0 + jnp.tanh(0.5 * v))
        hidden[:, pl.ds(pl.multiple_of(which * half, half), half)] = v.astype(BF16)
        at = pl.ds(pl.multiple_of(which * out_half, out_half), out_half)
        for d in range(members):
            for i in range(pieces):
                w_last[pl.ds(d * rows + i * step, step), at] = w[
                    d, rows:, i * out_half : (i + 1) * out_half
                ]
    embedding = jnp.dot(hidden[...], w_last[...], preferred_element_type=F32)
    norm = lax.rsqrt(jnp.sum(embedding * embedding, axis=1, keepdims=True) + 1e-06)
    unit[...] = (embedding * norm).astype(BF16)
    count = queries.shape[0]
    high = (positives[...] // 128).astype(F32)
    low = (positives[...] % 128).astype(F32)
    line = lax.broadcasted_iota(I32, (out.shape[1] - count, count), 0)
    tail = jnp.where(line == 0, high, jnp.where(line == 1, low, 0.0)).astype(BF16)
    for k in range(out.shape[0]):
        out[k, :count, :] = unit[...]
        out[k, count:, :] = tail


def scores_kernel(shared, box_own, box_other, out):
    core = core_index()
    x = x_index()
    chips = box_own.shape[0]
    part = box_own.shape[1] - 8
    local = chips * part
    count = out.shape[2]
    scale = 16.0 * math.log2(math.e)
    number = lax.broadcasted_iota(I32, (local, count), 0)
    banks = [b[:, :part, :].reshape(local, b.shape[2]) for b in (box_own, box_other)]
    for k in range(shared.shape[0]):
        query = shared[k, :count, :]
        tail = shared[k, count : count + 16, :].astype(F32)
        high, low = tail[0:1, :].astype(I32), tail[1:2, :].astype(I32)
        dots = [
            lax.dot_general(b, query, (((1,), (1,)), ((), ())), preferred_element_type=F32) for b in banks
        ]
        top = jnp.maximum(*[jnp.max(d, axis=0, keepdims=True) for d in dots])
        total = jnp.zeros_like(top)
        picked = jnp.zeros_like(top)
        for d, which in zip(dots, (core, 1 - core)):
            total += jnp.sum(jnp.exp2((d - top) * scale), axis=0, keepdims=True)
            mine = (high % CORES == which) & (low // part == x)
            at = jnp.where(mine, (high // CORES) * part + low % part, -1)
            picked += jnp.sum(jnp.where(number == at, d, 0.0), axis=0, keepdims=True)
        line = lax.broadcasted_iota(I32, (out.shape[1], count), 0)
        out[k, :, :] = jnp.where(
            line == 0, 16.0 * top, jnp.where(line == 1, total, jnp.where(line == 2, 16.0 * picked, 0.0))
        )


def loss_kernel(parts, out):
    top = jnp.max(parts[:, 0, :], axis=0, keepdims=True)
    total = jnp.sum(parts[:, 1, :] * jnp.exp(parts[:, 0, :] - top), axis=0, keepdims=True)
    out[...] = jnp.log(total) + top - jnp.sum(parts[:, 2, :], axis=0, keepdims=True)


def bank_kernel(box_own, box_other, bank, out):
    core = core_index()
    chips = box_own.shape[0]
    part = box_own.shape[1] - 8
    count = bank.shape[0]
    line = lax.broadcasted_iota(I32, (chips * 8, count), 0)
    kind = line % 8
    mine = (kind < 4) & ((kind // 2) == core)
    place = lax.broadcasted_iota(I32, (chips * 8, count), 1).astype(F32)
    keys, rows = [], []
    for box, source in ((box_own, core), (box_other, 1 - core)):
        block = box[:, part:, :].astype(F32)
        moved = jnp.concatenate([block[:, 4:, :], block[:, :4, :]], axis=1)
        slot = moved.reshape(chips * 8, block.shape[2])[:, :count]
        order = (line // 8) * 4 + source * 2 + kind % 2
        keys.append(jnp.where(mine & (slot == place), order, -1))
        rows.append(box[:, part:, :].reshape(chips * 8, block.shape[2]))
    winner = jnp.maximum(*[jnp.max(k, axis=0, keepdims=True) for k in keys])
    written = jnp.zeros(bank.shape, F32)
    found = jnp.zeros((count, 128), F32)
    for key, row in zip(keys, rows):
        chosen = jnp.where((key == winner) & (key >= 0), 1.0, 0.0).astype(BF16)
        contract = (((0,), (0,)), ((), ()))
        written += lax.dot_general(chosen, row, contract, preferred_element_type=F32)
        ones = jnp.ones((chips * 8, 128), BF16)
        found += lax.dot_general(chosen, ones, contract, preferred_element_type=F32)
    out[...] = jnp.where(found[:, :1] > 0.5, written, bank[...].astype(F32)).astype(BF16)


def body(queries, w_input, w_output, item_bank, positives, fresh_rows, owners, slots):
    sds = jax.ShapeDtypeStruct
    count = queries.shape[0]
    members = lax.axis_size("dp")
    chips = lax.axis_size("bank") // CORES
    part = item_bank.shape[0] // X
    width = item_bank.shape[1]
    half = w_input.shape[1] // CORES
    extra = w_output.size // CORES // half

    planes = [[k * CORES + c for k in range(chips)] for c in range(CORES)]
    rings = [[r * X + i for i in range(X)] for r in range(members // X)]
    swap = [(i, i ^ 1) for i in range(chips * CORES)]

    def exchange(a, axis, groups=None):
        return lax.all_to_all(a, axis, 0, 0, axis_index_groups=groups, tiled=True)

    w_send = call(
        weights_kernel, sds((members, w_input.shape[0] + extra, half), BF16), (w_input, w_output)
    )
    w_own = exchange(w_send, "dp")
    box_send = call(
        outbox_kernel,
        sds((chips, part + 8, width), BF16),
        (owners.reshape(1, -1), slots.reshape(1, -1), fresh_rows, item_bank),
    )
    box_send, w_own = lax.optimization_barrier((box_send, w_own))
    w_other = lax.ppermute(w_own, "bank", swap)
    box_own = exchange(box_send, "bank", planes)
    shared = call(
        tower_kernel,
        sds((X, count + 16, width), BF16),
        (queries, w_own, w_other, positives.reshape(1, -1)),
        [
            VMEM((count, w_input.shape[1]), BF16),
            VMEM((members * w_output.shape[0], width), BF16),
            VMEM((count, width), BF16),
        ],
    )
    box_own, shared = lax.optimization_barrier((box_own, shared))
    box_other = lax.ppermute(box_own, "bank", swap)
    shared = exchange(shared, "dp", rings)
    parts = call(scores_kernel, sds((X, 8, count), F32), (shared, box_own, box_other))
    parts = exchange(parts, "dp", rings)
    contrast_loss = call(loss_kernel, sds((1, count), F32), (parts,)).reshape(count)
    next_bank = call(bank_kernel, sds(item_bank.shape, BF16), (box_own, box_other, item_bank))
    return contrast_loss, next_bank


def solution(mesh):
    return jax.shard_map(
        body,
        mesh=mesh,
        in_specs=(
            P(("bank", "dp"), None),
            P("dp", None),
            P("dp", None),
            P("bank", None),
            P(("bank", "dp")),
            P("bank", None),
            P("bank", None),
            P("bank"),
        ),
        out_specs=(P(("bank", "dp")), P("bank", None)),
        check_vma=False,
    )
```

```python
import functools
import math

import jax
import jax.numpy as jnp
from jax import lax
from jax.experimental import pallas as pl
from jax.experimental.pallas import tpu as pltpu
from jax.sharding import PartitionSpec as P

BF16 = jnp.bfloat16
F32 = jnp.float32
I32 = jnp.int32

CORES = 2
X = 4
Y_LO = 4
Y = 8

VMEM = pltpu.VMEM
LIMIT = 48 * 1024 * 1024


def core_index():
    return lax.rem(lax.axis_index("bank"), CORES)


def y_lo_index():
    return lax.rem(lax.div(lax.axis_index("bank"), CORES), Y_LO)


def along_y(devices, members, moves):
    pairs = []
    for b in range(devices):
        for d in range(members):
            z, lo, core = b // (Y_LO * CORES), b // CORES % Y_LO, b % CORES
            hi, x = d // X, d % X
            y = moves[core][hi * Y_LO + lo] % Y
            to = ((z * Y_LO + y % Y_LO) * CORES + core) * members + y // Y_LO * X + x
            pairs.append((b * members + d, to))
    return pairs


def call(kernel, outs, args, scratch=()):
    return pl.pallas_call(
        kernel,
        out_shape=outs,
        in_specs=[pl.BlockSpec(memory_space=VMEM)] * len(args),
        out_specs=jax.tree.map(lambda _: pl.BlockSpec(memory_space=VMEM), outs),
        scratch_shapes=list(scratch),
        compiler_params=pltpu.CompilerParams(vmem_limit_bytes=LIMIT),
    )(*args)


def weights_kernel(w_input, w_output, out):
    rows, width = w_input.shape
    unit = w_output.shape[0] // CORES
    tall = out.shape[0] - rows
    wide = w_output.shape[1]

    def write(core):
        picked = [w_input[:, j + core * unit : j + (core + 1) * unit] for j in range(0, width, CORES * unit)]
        out[:rows, :] = jnp.concatenate(picked, axis=1)
        for i in range(unit // tall):
            at = core * unit + i * tall
            out[rows:, i * wide : (i + 1) * wide] = w_output[at : at + tall, :]

    for core in range(CORES):
        pl.when(core_index() == core)(functools.partial(write, core))


def outbox_kernel(owners, slots, fresh, bank, out):
    part = bank.shape[0]
    ring = out.shape[0]
    chips = ring * Y_LO
    for z in range(ring):
        out[z, :part, :] = bank[...]
    count = fresh.shape[0]
    owner = owners[...].astype(F32)
    across = jnp.broadcast_to(owner, (count, count))
    earlier = lax.broadcasted_iota(I32, (count, count), 0) < lax.broadcasted_iota(I32, (count, count), 1)
    same = across == across.T
    placed = jnp.sum(jnp.where(same & earlier, 1.0, 0.0), axis=0, keepdims=True)
    key = (owner * 2.0 + placed).astype(I32)
    row = lax.broadcasted_iota(I32, (chips * 8, count), 0)
    wanted = (row // 8) * 4 + (row % 4)
    chosen = wanted == key
    data = jnp.dot(chosen.astype(BF16), fresh[...], preferred_element_type=F32)
    slot = jnp.sum(jnp.where(chosen, slots[...].astype(F32) + 1.0, 0.0), axis=1, keepdims=True) - 1.0
    kind = lax.broadcasted_iota(I32, data.shape, 0) % 8
    both = jnp.where(kind < 4, data, slot).astype(BF16)
    out[:, part:, :] = both.reshape(ring, Y_LO * 8, both.shape[1])


def join_kernel(own, other, out):
    rows = own.shape[0]
    out[:rows, :] = own[...]
    out[rows:, :] = other[...]


def tower_kernel(q_own, q_other, w0, w1, w2, w3, positives, out, first, last):
    d = lax.axis_index("dp")
    x, y_hi = lax.rem(d, X), lax.div(d, X)
    count, depth = q_own.shape
    wide = out.shape[1]
    members = lax.axis_size("dp")
    rows = depth // members
    both = w0.shape[0] // 2
    tall = both - rows
    unit = tall * (w0.shape[1] // wide)
    for delta, w in enumerate((w0, w1, w2, w3)):
        for swapped in range(2):
            hi = jnp.where(swapped == 1, 1 - y_hi, y_hi)
            source = hi * X + lax.rem(x - delta + X, X)
            base = swapped * both
            first[pl.ds(pl.multiple_of(source * rows, rows), rows), :] = w[base : base + rows, :]
            for i in range(unit // tall):
                at = pl.multiple_of(source * unit + i * tall, tall)
                last[pl.ds(at, tall), :] = w[base + rows : base + both, i * wide : (i + 1) * wide]
    for i, q in enumerate((q_own, q_other)):
        v = jnp.dot(q[...], first[...], preferred_element_type=F32)
        v = (0.5 * v) * (1.0 + jnp.tanh(0.5 * v))
        out[i * count : (i + 1) * count, :] = jnp.dot(
            v.astype(BF16), last[...], preferred_element_type=F32
        )
    out[CORES * count :, :] = jnp.broadcast_to(positives[...].astype(F32), (8, wide))


def pick(box, part, which):
    rows = [box[:, part + 8 * j : part + 8 * (j + 1), :] for j in range(Y_LO)]
    out = rows[0]
    for j in range(1, Y_LO):
        out = jnp.where(which == j, rows[j], out)
    return out


def spread_kernel(box, *outs):
    y_lo = y_lo_index()
    part = outs[0].shape[1] - 8
    for i, out in enumerate(outs):
        out[:, :part, :] = box[:, :part, :]
        out[:, part:, :] = pick(box, part, lax.rem(y_lo + i + 1, Y_LO))


def scores_kernel(mine, received, b0, b1, b2, b3, keep, send):
    core, y_lo = core_index(), y_lo_index()
    count = keep.shape[1]
    ring = b1.shape[0]
    part = b1.shape[1] - 8
    scale = 16.0 * math.log2(math.e)
    local = ring * part
    number = lax.broadcasted_iota(I32, (local, count), 0)
    line = lax.broadcasted_iota(I32, (8, count), 0)
    for i, (place, out) in enumerate(((mine, keep), (received, send))):
        j = 1 - i
        embedding = mine[i * count : (i + 1) * count, :] + received[j * count : (j + 1) * count, :]
        norm = lax.rsqrt(jnp.sum(embedding * embedding, axis=1, keepdims=True) + 1e-06)
        unit = (embedding * norm).astype(BF16)
        positive = place[CORES * count : CORES * count + 1, :].astype(I32)
        block = positive // part
        chip = block // CORES
        away = (y_lo - chip % Y_LO + Y_LO) % Y_LO
        at = (chip // Y_LO) * part + positive % part
        at = jnp.where(block % CORES == core, at, -1)
        top = total = picked = None
        for delta, box in enumerate((b0, b1, b2, b3)):
            bank = box[:, :part, :].reshape(local, box.shape[2])
            d = lax.dot_general(bank, unit, (((1,), (1,)), ((), ())), preferred_element_type=F32)
            high = jnp.max(d, axis=0, keepdims=True)
            hit = number == jnp.where(away == delta, at, -1)
            here = jnp.sum(jnp.where(hit, d, 0.0), axis=0, keepdims=True)
            if top is None:
                top, picked = high, here
                total = jnp.sum(jnp.exp2((d - top) * scale), axis=0, keepdims=True)
            else:
                old, top = top, jnp.maximum(top, high)
                total = total * jnp.exp2((old - top) * scale)
                total += jnp.sum(jnp.exp2((d - top) * scale), axis=0, keepdims=True)
                picked += here
        out[:8, :] = jnp.where(
            line == 0, 16.0 * top, jnp.where(line == 1, total, jnp.where(line == 2, 16.0 * picked, 0.0))
        )
    blocks = [pick(b0, part, y_lo)] + [b[:, part:, :] for b in (b1, b2, b3)]
    for i, block in enumerate(blocks):
        fresh = block.reshape(ring * 8, block.shape[2]).astype(F32)
        for out in (keep, send):
            out[8 + i * ring * 8 : 8 + (i + 1) * ring * 8, :] = fresh


def last_kernel(keep, got, bank, loss, next_bank):
    tops = [keep[0:1, :], got[0:1, :]]
    top = jnp.maximum(*tops)
    total = sum(s[1:2, :] * jnp.exp(t - top) for s, t in zip((keep, got), tops))
    loss[...] = jnp.log(total) + top - (keep[2:3, :] + got[2:3, :])

    core, y_lo = core_index(), y_lo_index()
    count, wide = bank.shape
    lines = keep.shape[0] - 8
    ring = lines // (8 * Y_LO)
    line = lax.broadcasted_iota(I32, (lines, count), 0)
    kind = line % 8
    mine = (kind < 4) & ((kind // 2) == core)
    chip = (line // 8 % ring) * Y_LO + (y_lo + Y_LO - line // (8 * ring)) % Y_LO
    place = lax.broadcasted_iota(I32, (lines, count), 1).astype(F32)
    keys, rows = [], []
    for source, ref in ((core, keep), (1 - core, got)):
        block = ref[8:, :].reshape(lines // 8, 8, wide)
        slot = jnp.concatenate([block[:, 4:, :count], block[:, :4, :count]], axis=1)
        slot = slot.reshape(lines, count)
        order = chip * 4 + source * 2 + kind % 2
        keys.append(jnp.where(mine & (slot == place), order, -1))
        rows.append(ref[8:, :].astype(BF16))
    winner = jnp.maximum(*[jnp.max(k, axis=0, keepdims=True) for k in keys])
    written = jnp.zeros(bank.shape, F32)
    found = jnp.zeros((count, 128), F32)
    for key, row in zip(keys, rows):
        chosen = jnp.where((key == winner) & (key >= 0), 1.0, 0.0).astype(BF16)
        contract = (((0,), (0,)), ((), ()))
        written += lax.dot_general(chosen, row, contract, preferred_element_type=F32)
        ones = jnp.ones((lines, 128), BF16)
        found += lax.dot_general(chosen, ones, contract, preferred_element_type=F32)
    next_bank[...] = jnp.where(found[:, :1] > 0.5, written, bank[...].astype(F32)).astype(BF16)


def body(queries, w_input, w_output, item_bank, positives, fresh_rows, owners, slots):
    sds = jax.ShapeDtypeStruct
    count = queries.shape[0]
    members = lax.axis_size("dp")
    devices = lax.axis_size("bank")
    chips = devices // CORES
    ring = chips // Y_LO
    part, width = item_bank.shape
    half = w_input.shape[1] // CORES
    tall = w_input.shape[0] + w_output.size // CORES // half

    columns = [[z * Y_LO * CORES + i for z in range(ring)] for i in range(Y_LO * CORES)]
    swap = [(i, i ^ 1) for i in range(devices)]

    def around(a, delta):
        return lax.ppermute(
            a, "dp", [(i, i // X * X + (i % X + delta) % X) for i in range(members)]
        )

    def move_y(a, to):
        return lax.ppermute(a, ("bank", "dp"), along_y(devices, members, to))

    box_send = call(
        outbox_kernel,
        sds((ring, part + Y_LO * 8, width), BF16),
        (owners.reshape(1, -1), slots.reshape(1, -1), fresh_rows, item_bank),
    )
    box = lax.all_to_all(box_send, "bank", 0, 0, axis_index_groups=columns, tiled=True)
    w_mine = call(weights_kernel, sds((tall, half), BF16), (w_input, w_output))
    w_swapped = move_y(w_mine, [[6, 7, 4, 5, 2, 3, 0, 1]] * CORES)
    q_other = lax.ppermute(queries, "bank", swap)
    boxes = call(spread_kernel, (sds((ring, part + 8, width), BF16),) * 3, (box,))
    boxes = [
        move_y(b, [[y + step for y in range(Y)] for step in steps])
        for b, steps in zip(boxes, ((1, 1), (2, -2), (-1, -1)))
    ]
    w_both = call(join_kernel, sds((2 * tall, half), BF16), (w_mine, w_swapped))
    weights = [w_both] + [around(w_both, delta) for delta in range(1, X)]
    mine = call(
        tower_kernel,
        sds((CORES * count + 8, width), F32),
        (queries, q_other, *weights, positives.reshape(1, -1)),
        [VMEM((w_input.shape[1], half), BF16), VMEM((half, width), BF16)],
    )
    received = lax.ppermute(mine, "bank", swap)
    keep, send = call(
        scores_kernel, (sds((8 + chips * 8, width), F32),) * 2, (mine, received, box, *boxes)
    )
    got = lax.ppermute(send, "bank", swap)
    loss, next_bank = call(
        last_kernel,
        (sds((1, count), F32), sds(item_bank.shape, BF16)),
        (keep, got, item_bank),
    )
    return loss.reshape(count), next_bank


def solution(mesh):
    return jax.shard_map(
        body,
        mesh=mesh,
        in_specs=(
            P(("bank", "dp"), None),
            P("dp", None),
            P("dp", None),
            P("bank", None),
            P(("bank", "dp")),
            P("bank", None),
            P("bank", None),
            P("bank"),
        ),
        out_specs=(P(("bank", "dp")), P("bank", None)),
        check_vma=False,
    )
```

```python
import functools
import math

import jax
import jax.numpy as jnp
from jax import lax
from jax.experimental import pallas as pl
from jax.experimental.pallas import tpu as pltpu
from jax.sharding import PartitionSpec as P

BF16 = jnp.bfloat16
F32 = jnp.float32
I32 = jnp.int32

CORES = 2
X = 4
Y_LO = 4
Y = 8

VMEM = pltpu.VMEM
LIMIT = 48 * 1024 * 1024
MOST = 60 * 1024 * 1024
SMALL = pl.CostEstimate(flops=1 << 10, bytes_accessed=1 << 10, transcendentals=0)
LARGE = pl.CostEstimate(flops=1 << 36, bytes_accessed=1 << 10, transcendentals=0)


def core_index():
    return lax.rem(lax.axis_index("bank"), CORES)


def y_lo_index():
    return lax.rem(lax.div(lax.axis_index("bank"), CORES), Y_LO)


def half_index():
    return lax.rem(lax.rem(lax.axis_index("dp"), X) + core_index(), 2)


def to_partner(devices, members):
    pairs = []
    for b in range(devices):
        for d in range(members):
            x = d % X
            other = (x + 1 if (x + b) % 2 == 0 else x - 1) % X
            pairs.append((b * members + d, b * members + d - x + other))
    return pairs


def along_y(devices, members, moves):
    pairs = []
    for b in range(devices):
        for d in range(members):
            z, lo, core = b // (Y_LO * CORES), b // CORES % Y_LO, b % CORES
            hi, x = d // X, d % X
            y = moves[core][hi * Y_LO + lo] % Y
            to = ((z * Y_LO + y % Y_LO) * CORES + core) * members + y // Y_LO * X + x
            pairs.append((b * members + d, to))
    return pairs


def call(kernel, outs, args, scratch=(), ins=VMEM, space=None, limit=LIMIT, cost=SMALL):
    space = space or jax.tree.map(lambda _: VMEM, outs)
    return pl.pallas_call(
        kernel,
        out_shape=outs,
        in_specs=[pl.BlockSpec(memory_space=ins)] * len(args),
        out_specs=jax.tree.map(lambda _, s: pl.BlockSpec(memory_space=s), outs, space),
        scratch_shapes=list(scratch),
        cost_estimate=cost,
        compiler_params=pltpu.CompilerParams(vmem_limit_bytes=limit),
    )(*args)


def weights_kernel(w_input_in, w_output_in, half, w_input, w_output, sems):
    loads = [
        pltpu.make_async_copy(a, b, sems.at[i])
        for i, (a, b) in enumerate(((w_input_in, w_input), (w_output_in, w_output)))
    ]
    for copy in loads:
        copy.start()
    for copy in loads:
        copy.wait()
    tall, width = w_input.shape
    unit = w_output.shape[0] // CORES
    step = half.shape[0] - tall
    wide = w_output.shape[1]

    def write(core):
        picked = [w_input[:, j + core * unit : j + (core + 1) * unit] for j in range(0, width, CORES * unit)]
        half[:tall, :] = jnp.concatenate(picked, axis=1)
        for i in range(unit // step):
            at = core * unit + i * step
            half[tall:, i * wide : (i + 1) * wide] = w_output[at : at + step, :]

    for core in range(CORES):
        pl.when(core_index() == core)(functools.partial(write, core))


def outbox_kernel(owners_in, slots_in, fresh_in, bank_in, out, owners, slots, fresh, bank, rows, sems):
    part = bank.shape[0]
    ring = out.shape[0]
    at = pl.multiple_of(half_index() * part, part)
    loads = [
        pltpu.make_async_copy(a, b, sems.at[i])
        for i, (a, b) in enumerate(
            (
                (bank_in.at[pl.ds(at, part)], bank),
                (owners_in, owners),
                (slots_in, slots),
                (fresh_in, fresh),
            )
        )
    ]
    blocks = [pltpu.make_async_copy(bank, out.at[z, pl.ds(0, part)], sems.at[5 + z]) for z in range(ring)]
    for copy in loads:
        copy.start()
    loads[0].wait()
    for copy in blocks:
        copy.start()
    for copy in loads[1:]:
        copy.wait()
    count = fresh.shape[0]
    owner = owners[...].astype(F32)
    across = jnp.broadcast_to(owner, (count, count))
    earlier = lax.broadcasted_iota(I32, (count, count), 0) < lax.broadcasted_iota(I32, (count, count), 1)
    same = across == across.T
    placed = jnp.sum(jnp.where(same & earlier, 1.0, 0.0), axis=0, keepdims=True)
    key = (owner * 2.0 + placed).astype(I32)
    row = lax.broadcasted_iota(I32, (ring * Y_LO * 8, count), 0)
    wanted = (row // 8) * 4 + (row % 4)
    chosen = wanted == key
    data = jnp.dot(chosen.astype(BF16), fresh[...], preferred_element_type=F32)
    slot = jnp.sum(jnp.where(chosen, slots[...].astype(F32) + 1.0, 0.0), axis=1, keepdims=True) - 1.0
    kind = lax.broadcasted_iota(I32, data.shape, 0) % 8
    both = jnp.where(kind < 4, data, slot).astype(BF16)
    rows[...] = both.reshape(rows.shape)
    store = pltpu.make_async_copy(rows, out.at[:, pl.ds(part, rows.shape[1])], sems.at[4])
    store.start()
    for copy in (*blocks, store):
        copy.wait()


def join_kernel(own, other, out):
    rows = own.shape[0]
    out[:rows, :] = own[...]
    out[rows:, :] = other[...]


def tower_kernel(q_own, q_other, w0, w1, w2, w3, positives, out, first, last):
    d = lax.axis_index("dp")
    x, y_hi = lax.rem(d, X), lax.div(d, X)
    count, depth = q_own.shape
    wide = out.shape[1]
    members = lax.axis_size("dp")
    rows = depth // members
    both = w0.shape[0] // 2
    tall = both - rows
    unit = tall * (w0.shape[1] // wide)
    for delta, w in enumerate((w0, w1, w2, w3)):
        for swapped in range(2):
            hi = jnp.where(swapped == 1, 1 - y_hi, y_hi)
            source = hi * X + lax.rem(x + X - away_of(delta), X)
            base = swapped * both
            first[pl.ds(pl.multiple_of(source * rows, rows), rows), :] = w[base : base + rows, :]
            for i in range(unit // tall):
                at = pl.multiple_of(source * unit + i * tall, tall)
                last[pl.ds(at, tall), :] = w[base + rows : base + both, i * wide : (i + 1) * wide]
    for i, q in enumerate((q_own, q_other)):
        v = jnp.dot(q[...], first[...], preferred_element_type=F32)
        v = (0.5 * v) * (1.0 + jnp.tanh(0.5 * v))
        out[i * count : (i + 1) * count, :] = jnp.dot(
            v.astype(BF16), last[...], preferred_element_type=F32
        )
    out[CORES * count :, :] = jnp.broadcast_to(positives[...].astype(F32), (8, wide))


def away_of(i):
    return jnp.where(core_index() == 0, i, (4 - i) % 4)


def pick(box, part, which):
    rows = [box[:, part + 8 * j : part + 8 * (j + 1), :] for j in range(Y_LO)]
    out = rows[0]
    for j in range(1, Y_LO):
        out = jnp.where(which == j, rows[j], out)
    return out


def two_kernel(box, out):
    y_lo = y_lo_index()
    part = out.shape[1] - 16
    out[:, :part, :] = box[:, :part, :]
    fresh = [pick(box, part, lax.rem(y_lo + away_of(i), Y_LO)) for i in (2, 3)]
    out[:, part:, :] = jnp.concatenate(fresh, axis=1)


def one_kernel(box, two, out):
    part = two.shape[1] - 16
    out[:, :part, :] = box[:, :part, :]
    out[:, part : 2 * part, :] = two[:, :part, :]
    own = pick(box, part, lax.rem(y_lo_index() + away_of(1), Y_LO))
    out[:, 2 * part :, :] = jnp.concatenate([own, two[:, part + 8 :, :]], axis=1)


def unit_kernel(mine, received, out):
    count = (mine.shape[0] - 8) // CORES
    line = lax.broadcasted_iota(I32, (16, mine.shape[1]), 0)
    tail = jnp.zeros(line.shape, F32)
    for i, place in enumerate((mine, received)):
        j = 1 - i
        embedding = mine[i * count : (i + 1) * count, :] + received[j * count : (j + 1) * count, :]
        norm = lax.rsqrt(jnp.sum(embedding * embedding, axis=1, keepdims=True) + 1e-06)
        out[i * count : (i + 1) * count, :] = (embedding * norm).astype(BF16)
        positive = place[CORES * count : CORES * count + 1, :].astype(I32)
        tail = jnp.where(line == 2 * i, (positive // 128).astype(F32), tail)
        tail = jnp.where(line == 2 * i + 1, (positive % 128).astype(F32), tail)
    out[CORES * count :, :] = tail.astype(BF16)


def score_kernel(far, units, *refs):
    out = refs[-1]
    old = refs[0] if far else None
    core, y_lo, half = core_index(), y_lo_index(), half_index()
    ring, count = refs[1].shape[0], out.shape[1]
    part = (refs[1].shape[1] - 16) // (2 if far else 1)
    boxes = ((1, refs[1], 0), (3, refs[1], part)) if far else ((0, refs[0], 0), (2, refs[1], 0))
    scale = 16.0 * math.log2(math.e)
    local = ring * part
    number = lax.broadcasted_iota(I32, (local, count), 0)
    line = lax.broadcasted_iota(I32, (8, count), 0)
    tail = units[CORES * count :, :].astype(F32)
    for i in range(CORES):
        unit = units[i * count : (i + 1) * count, :]
        block = tail[2 * i : 2 * i + 1, :].astype(I32)
        row = tail[2 * i + 1 : 2 * i + 2, :].astype(I32)
        chip = block // CORES
        away = (y_lo - chip % Y_LO + Y_LO) % Y_LO
        at = (chip // Y_LO) * part + row % part
        at = jnp.where((block % CORES == core) & (row // part == half), at, -1)
        top = total = picked = None
        if old is not None:
            top, total, picked = (old[8 * i + k : 8 * i + k + 1, :] for k in range(3))
        for delta, box, base in boxes:
            bank = box[:, base : base + part, :].reshape(local, box.shape[2])
            d = lax.dot_general(bank, unit, (((1,), (1,)), ((), ())), preferred_element_type=F32)
            high = jnp.max(d, axis=0, keepdims=True)
            hit = number == jnp.where(away == away_of(delta), at, -1)
            here = jnp.sum(jnp.where(hit, d, 0.0), axis=0, keepdims=True)
            if top is None:
                top, picked = high, here
                total = jnp.sum(jnp.exp2((d - top) * scale), axis=0, keepdims=True)
            else:
                before, top = top, jnp.maximum(top, high)
                total = total * jnp.exp2((before - top) * scale)
                total += jnp.sum(jnp.exp2((d - top) * scale), axis=0, keepdims=True)
                picked += here
        out[8 * i : 8 * i + 8, :] = jnp.where(
            line == 0, top, jnp.where(line == 1, total, jnp.where(line == 2, picked, 0.0))
        )


def merge_kernel(state, back, b0, b2, b1, keep, send):
    line = lax.broadcasted_iota(I32, (8, state.shape[1]), 0)
    scale = 16.0 * math.log2(math.e)
    for i, out in enumerate((keep, send)):
        a, b = state[8 * i : 8 * i + 8, :], back[8 * i : 8 * i + 8, :]
        top = jnp.maximum(a[0:1, :], b[0:1, :])
        total = sum(s[1:2, :] * jnp.exp2((s[0:1, :] - top) * scale) for s in (a, b))
        out[:8, :] = jnp.where(line == 0, top, jnp.where(line == 1, total, a + b))
    ring, width = b2.shape[0], b2.shape[2]
    part = b2.shape[1] - 16
    blocks = [
        pick(b0, part, y_lo_index()),
        b1[:, 2 * part : 2 * part + 8, :],
        b2[:, part : part + 8, :],
        b1[:, 2 * part + 8 :, :],
    ]
    for i, block in enumerate(blocks):
        fresh = block.reshape(ring * 8, width).astype(F32)
        for out in (keep, send):
            out[8 + i * ring * 8 : 8 + (i + 1) * ring * 8, :] = fresh


def last_kernel(keep, got, bank, loss, next_bank):
    tops = [keep[0:1, :], got[0:1, :]]
    top = jnp.maximum(*tops)
    total = sum(s[1:2, :] * jnp.exp(16.0 * (t - top)) for s, t in zip((keep, got), tops))
    loss[...] = jnp.log(total) + 16.0 * (top - (keep[2:3, :] + got[2:3, :]))

    core, y_lo = core_index(), y_lo_index()
    count, wide = bank.shape
    lines = keep.shape[0] - 8
    ring = lines // (8 * Y_LO)
    line = lax.broadcasted_iota(I32, (lines, count), 0)
    kind = line % 8
    mine = (kind < 4) & ((kind // 2) == core)
    group = line // (8 * ring)
    place = lax.broadcasted_iota(I32, (lines, count), 1).astype(F32)
    keys, rows = [], []
    for source, ref in ((core, keep), (1 - core, got)):
        block = ref[8:, :].reshape(lines // 8, 8, wide)
        slot = jnp.concatenate([block[:, 4:, :count], block[:, :4, :count]], axis=1)
        slot = slot.reshape(lines, count)
        away = jnp.where(source == 0, group, (Y_LO - group) % Y_LO)
        chip = (line // 8 % ring) * Y_LO + (y_lo + Y_LO - away) % Y_LO
        order = chip * 4 + source * 2 + kind % 2
        keys.append(jnp.where(mine & (slot == place), order, -1))
        rows.append(ref[8:, :].astype(BF16))
    winner = jnp.maximum(*[jnp.max(k, axis=0, keepdims=True) for k in keys])
    written = jnp.zeros(bank.shape, F32)
    found = jnp.zeros((count, 128), F32)
    for key, row in zip(keys, rows):
        chosen = jnp.where((key == winner) & (key >= 0), 1.0, 0.0).astype(BF16)
        contract = (((0,), (0,)), ((), ()))
        written += lax.dot_general(chosen, row, contract, preferred_element_type=F32)
        ones = jnp.ones((lines, 128), BF16)
        found += lax.dot_general(chosen, ones, contract, preferred_element_type=F32)
    next_bank[...] = jnp.where(found[:, :1] > 0.5, written, bank[...].astype(F32)).astype(BF16)


def body(queries, w_input, w_output, item_bank, positives, fresh_rows, owners, slots):
    sds = jax.ShapeDtypeStruct
    count = queries.shape[0]
    members = lax.axis_size("dp")
    devices = lax.axis_size("bank")
    chips = devices // CORES
    ring = chips // Y_LO
    part, width = item_bank.shape[0] // 2, item_bank.shape[1]
    half = w_input.shape[1] // CORES
    tall = w_input.shape[0] + w_output.size // CORES // half

    columns = [[z * Y_LO * CORES + i for z in range(ring)] for i in range(Y_LO * CORES)]
    swap = [(i, i ^ 1) for i in range(devices)]

    def around(a, delta):
        pairs = []
        for i in range(devices * members):
            x, up = i % X, i // members % CORES == 0
            pairs.append((i, i - x + (x + (delta if up else -delta)) % X))
        return lax.ppermute(a, ("bank", "dp"), pairs)

    def move_y(a, to):
        return lax.ppermute(a, ("bank", "dp"), along_y(devices, members, to))

    w_mine = call(
        weights_kernel,
        sds((tall, half), BF16),
        (w_input, w_output),
        [VMEM(w_input.shape, BF16), VMEM(w_output.shape, BF16), pltpu.SemaphoreType.DMA((2,))],
        ins=pl.ANY,
        limit=MOST,
    )
    box_send = call(
        outbox_kernel,
        sds((ring, part + Y_LO * 8, width), BF16),
        (owners.reshape(1, -1), slots.reshape(1, -1), fresh_rows, item_bank),
        [
            VMEM((1, owners.shape[0]), I32),
            VMEM((1, slots.shape[0]), I32),
            VMEM(fresh_rows.shape, BF16),
            VMEM((part, width), BF16),
            VMEM((ring, Y_LO * 8, width), BF16),
            pltpu.SemaphoreType.DMA((5 + ring,)),
        ],
        ins=pl.ANY,
        space=pl.ANY,
        limit=MOST,
    )
    b0 = lax.all_to_all(box_send, "bank", 0, 0, axis_index_groups=columns, tiled=True)
    w_swapped = move_y(w_mine, [[6, 7, 4, 5, 2, 3, 0, 1]] * CORES)
    q_other = lax.ppermute(queries, "bank", swap)
    b2 = call(two_kernel, sds((ring, part + 16, width), BF16), (b0,))
    b2 = move_y(b2, [[y + step for y in range(Y)] for step in (2, -2)])
    b1 = call(one_kernel, sds((ring, 2 * part + 16, width), BF16), (b0, b2))
    b1 = move_y(b1, [[y + step for y in range(Y)] for step in (1, -1)])
    w_both = call(join_kernel, sds((2 * tall, half), BF16), (w_mine, w_swapped), cost=LARGE)
    weights = [w_both] + [around(w_both, delta) for delta in range(1, X)]
    b0, q_other = lax.optimization_barrier((b0, q_other))
    mine = call(
        tower_kernel,
        sds((CORES * count + 8, width), F32),
        (queries, q_other, *weights, positives.reshape(1, -1)),
        [VMEM((w_input.shape[1], half), BF16), VMEM((half, width), BF16)],
    )
    received = lax.ppermute(mine, "bank", swap)
    units = call(unit_kernel, sds((CORES * count + 16, width), BF16), (mine, received))
    partners = lax.ppermute(units, ("bank", "dp"), to_partner(devices, members))

    def score(far, units, *refs):
        return call(
            functools.partial(score_kernel, far), sds((8 * CORES, count), F32), (units, *refs)
        )

    state = score(False, units, b0, b2)
    theirs = score(False, partners, b0, b2)
    theirs = score(True, partners, theirs, b1)
    back = lax.ppermute(theirs, ("bank", "dp"), to_partner(devices, members))
    state = score(True, units, state, b1)
    keep, send = call(
        merge_kernel,
        (sds((8 + chips * 8, width), F32),) * 2,
        (state, back, b0, b2, b1),
    )
    got = lax.ppermute(send, "bank", swap)
    loss, next_bank = call(
        last_kernel,
        (sds((1, count), F32), sds(item_bank.shape, BF16)),
        (keep, got, item_bank),
    )
    return loss.reshape(count), next_bank


def solution(mesh):
    return jax.shard_map(
        body,
        mesh=mesh,
        in_specs=(
            P(("bank", "dp"), None),
            P("dp", None),
            P("dp", None),
            P("bank", None),
            P(("bank", "dp")),
            P("bank", None),
            P("bank", None),
            P("bank"),
        ),
        out_specs=(P(("bank", "dp")), P("bank", None)),
        check_vma=False,
    )
```

```python
import functools
import math

import jax
import jax.numpy as jnp
from jax import lax
from jax.experimental import pallas as pl
from jax.experimental.pallas import tpu as pltpu
from jax.sharding import PartitionSpec as P

BF16 = jnp.bfloat16
F32 = jnp.float32
I32 = jnp.int32

CORES = 2
X = 4
Y_LO = 4
Y = 8

VMEM = pltpu.VMEM
LIMIT = 48 * 1024 * 1024
MOST = 60 * 1024 * 1024
SMALL = pl.CostEstimate(flops=1 << 10, bytes_accessed=1 << 10, transcendentals=0)
LARGE = pl.CostEstimate(flops=1 << 36, bytes_accessed=1 << 10, transcendentals=0)


def core_index():
    return lax.rem(lax.axis_index("bank"), CORES)


def y_lo_index():
    return lax.rem(lax.div(lax.axis_index("bank"), CORES), Y_LO)


def half_index():
    return lax.rem(lax.rem(lax.axis_index("dp"), X) + core_index(), 2)


def to_partner(devices, members):
    pairs = []
    for b in range(devices):
        for d in range(members):
            x = d % X
            other = (x + 1 if (x + b) % 2 == 0 else x - 1) % X
            pairs.append((b * members + d, b * members + d - x + other))
    return pairs


def along_y(devices, members, moves):
    pairs = []
    for b in range(devices):
        for d in range(members):
            z, lo, core = b // (Y_LO * CORES), b // CORES % Y_LO, b % CORES
            hi, x = d // X, d % X
            y = moves[core][hi * Y_LO + lo] % Y
            to = ((z * Y_LO + y % Y_LO) * CORES + core) * members + y // Y_LO * X + x
            pairs.append((b * members + d, to))
    return pairs


def call(kernel, outs, args, scratch=(), ins=VMEM, space=None, limit=LIMIT, cost=SMALL):
    space = space or jax.tree.map(lambda _: VMEM, outs)
    return pl.pallas_call(
        kernel,
        out_shape=outs,
        in_specs=[pl.BlockSpec(memory_space=ins)] * len(args),
        out_specs=jax.tree.map(lambda _, s: pl.BlockSpec(memory_space=s), outs, space),
        scratch_shapes=list(scratch),
        cost_estimate=cost,
        compiler_params=pltpu.CompilerParams(vmem_limit_bytes=limit),
    )(*args)


def first_kernel(
    w_input_in, w_output_in, owners_in, slots_in, fresh_in, bank_in,
    half, out, w_input, w_output, owners, slots, fresh, bank, rows, sems,
):
    part = bank.shape[0]
    ring = out.shape[0]
    at = pl.multiple_of(half_index() * part, part)
    loads = [
        pltpu.make_async_copy(a, b, sems.at[i])
        for i, (a, b) in enumerate(
            (
                (bank_in.at[pl.ds(at, part)], bank),
                (owners_in, owners),
                (slots_in, slots),
                (fresh_in, fresh),
                (w_input_in, w_input),
                (w_output_in, w_output),
            )
        )
    ]
    blocks = [pltpu.make_async_copy(bank, out.at[z, pl.ds(0, part)], sems.at[7 + z]) for z in range(ring)]
    for copy in loads:
        copy.start()
    loads[0].wait()
    for copy in blocks:
        copy.start()
    for copy in loads[1:4]:
        copy.wait()
    count = fresh.shape[0]
    owner = owners[...].astype(F32)
    across = jnp.broadcast_to(owner, (count, count))
    earlier = lax.broadcasted_iota(I32, (count, count), 0) < lax.broadcasted_iota(I32, (count, count), 1)
    same = across == across.T
    placed = jnp.sum(jnp.where(same & earlier, 1.0, 0.0), axis=0, keepdims=True)
    key = (owner * 2.0 + placed).astype(I32)
    row = lax.broadcasted_iota(I32, (ring * Y_LO * 8, count), 0)
    wanted = (row // 8) * 4 + (row % 4)
    chosen = wanted == key
    data = jnp.dot(chosen.astype(BF16), fresh[...], preferred_element_type=F32)
    slot = jnp.sum(jnp.where(chosen, slots[...].astype(F32) + 1.0, 0.0), axis=1, keepdims=True) - 1.0
    kind = lax.broadcasted_iota(I32, data.shape, 0) % 8
    both = jnp.where(kind < 4, data, slot).astype(BF16)
    rows[...] = both.reshape(rows.shape)
    store = pltpu.make_async_copy(rows, out.at[:, pl.ds(part, rows.shape[1])], sems.at[6])
    store.start()
    for copy in loads[4:]:
        copy.wait()
    tall, width = w_input.shape
    unit = w_output.shape[0] // CORES
    step = half.shape[0] - tall
    wide = w_output.shape[1]

    def write(core):
        picked = [w_input[:, j + core * unit : j + (core + 1) * unit] for j in range(0, width, CORES * unit)]
        half[:tall, :] = jnp.concatenate(picked, axis=1)
        for i in range(unit // step):
            at = core * unit + i * step
            half[tall:, i * wide : (i + 1) * wide] = w_output[at : at + step, :]

    for core in range(CORES):
        pl.when(core_index() == core)(functools.partial(write, core))
    for copy in (*blocks, store):
        copy.wait()


def join_kernel(own, other, out):
    rows = own.shape[0]
    out[:rows, :] = own[...]
    out[rows:, :] = other[...]


def tower_kernel(q_own, q_other, w0, w1, w2, w3, positives, out, first, last):
    d = lax.axis_index("dp")
    x, y_hi = lax.rem(d, X), lax.div(d, X)
    count, depth = q_own.shape
    wide = out.shape[1]
    members = lax.axis_size("dp")
    rows = depth // members
    both = w0.shape[0] // 2
    tall = both - rows
    unit = tall * (w0.shape[1] // wide)
    for delta, w in enumerate((w0, w1, w2, w3)):
        for swapped in range(2):
            hi = jnp.where(swapped == 1, 1 - y_hi, y_hi)
            source = hi * X + lax.rem(x + X - away_of(delta), X)
            base = swapped * both
            first[pl.ds(pl.multiple_of(source * rows, rows), rows), :] = w[base : base + rows, :]
            for i in range(unit // tall):
                at = pl.multiple_of(source * unit + i * tall, tall)
                last[pl.ds(at, tall), :] = w[base + rows : base + both, i * wide : (i + 1) * wide]
    for i, q in enumerate((q_own, q_other)):
        v = jnp.dot(q[...], first[...], preferred_element_type=F32)
        v = (0.5 * v) * (1.0 + jnp.tanh(0.5 * v))
        out[i * count : (i + 1) * count, :] = jnp.dot(
            v.astype(BF16), last[...], preferred_element_type=F32
        )
    out[CORES * count :, :] = jnp.broadcast_to(positives[...].astype(F32), (8, wide))


def away_of(i):
    return jnp.where(core_index() == 0, i, (4 - i) % 4)


def pick(box, part, which):
    rows = [box[:, part + 8 * j : part + 8 * (j + 1), :] for j in range(Y_LO)]
    out = rows[0]
    for j in range(1, Y_LO):
        out = jnp.where(which == j, rows[j], out)
    return out


def two_kernel(box, out):
    y_lo = y_lo_index()
    part = out.shape[1] - 16
    out[:, :part, :] = box[:, :part, :]
    fresh = [pick(box, part, lax.rem(y_lo + away_of(i), Y_LO)) for i in (2, 3)]
    out[:, part:, :] = jnp.concatenate(fresh, axis=1)


def one_kernel(box, two, out):
    part = two.shape[1] - 16
    out[:, :part, :] = box[:, :part, :]
    out[:, part : 2 * part, :] = two[:, :part, :]
    own = pick(box, part, lax.rem(y_lo_index() + away_of(1), Y_LO))
    out[:, 2 * part :, :] = jnp.concatenate([own, two[:, part + 8 :, :]], axis=1)


def unit_kernel(mine, received, out):
    count = (mine.shape[0] - 8) // CORES
    line = lax.broadcasted_iota(I32, (16, mine.shape[1]), 0)
    tail = jnp.zeros(line.shape, F32)
    for i, place in enumerate((mine, received)):
        j = 1 - i
        embedding = mine[i * count : (i + 1) * count, :] + received[j * count : (j + 1) * count, :]
        norm = lax.rsqrt(jnp.sum(embedding * embedding, axis=1, keepdims=True) + 1e-06)
        out[i * count : (i + 1) * count, :] = (embedding * norm).astype(BF16)
        positive = place[CORES * count : CORES * count + 1, :].astype(I32)
        tail = jnp.where(line == 2 * i, (positive // 128).astype(F32), tail)
        tail = jnp.where(line == 2 * i + 1, (positive % 128).astype(F32), tail)
    out[CORES * count :, :] = tail.astype(BF16)


def score_kernel(near, far, units, *refs):
    out = refs[-1]
    old = None if near else refs[0]
    core, y_lo, half = core_index(), y_lo_index(), half_index()
    ring, count = refs[1].shape[0], out.shape[1]
    part = refs[1].shape[1] - 16 if near else (refs[1].shape[1] - 16) // 2
    boxes = []
    if near:
        boxes += [(0, refs[0], 0), (2, refs[1], 0)]
    if far:
        boxes += [(1, refs[-2], 0), (3, refs[-2], part)]
    scale = 16.0 * math.log2(math.e)
    local = ring * part
    number = lax.broadcasted_iota(I32, (local, count), 0)
    line = lax.broadcasted_iota(I32, (8, count), 0)
    tail = units[CORES * count :, :].astype(F32)
    for i in range(CORES):
        unit = units[i * count : (i + 1) * count, :]
        block = tail[2 * i : 2 * i + 1, :].astype(I32)
        row = tail[2 * i + 1 : 2 * i + 2, :].astype(I32)
        chip = block // CORES
        away = (y_lo - chip % Y_LO + Y_LO) % Y_LO
        at = (chip // Y_LO) * part + row % part
        at = jnp.where((block % CORES == core) & (row // part == half), at, -1)
        top = total = picked = None
        if old is not None:
            top, total, picked = (old[8 * i + k : 8 * i + k + 1, :] for k in range(3))
        for delta, box, base in boxes:
            bank = box[:, base : base + part, :].reshape(local, box.shape[2])
            d = lax.dot_general(bank, unit, (((1,), (1,)), ((), ())), preferred_element_type=F32)
            high = jnp.max(d, axis=0, keepdims=True)
            hit = number == jnp.where(away == away_of(delta), at, -1)
            here = jnp.sum(jnp.where(hit, d, 0.0), axis=0, keepdims=True)
            if top is None:
                top, picked = high, here
                total = jnp.sum(jnp.exp2((d - top) * scale), axis=0, keepdims=True)
            else:
                before, top = top, jnp.maximum(top, high)
                total = total * jnp.exp2((before - top) * scale)
                total += jnp.sum(jnp.exp2((d - top) * scale), axis=0, keepdims=True)
                picked += here
        out[8 * i : 8 * i + 8, :] = jnp.where(
            line == 0, top, jnp.where(line == 1, total, jnp.where(line == 2, picked, 0.0))
        )


def fresh_kernel(b0, b2, b1, mine, theirs):
    core = core_index()
    ring, width = b2.shape[0], b2.shape[2]
    part = b2.shape[1] - 16
    blocks = [
        pick(b0, part, y_lo_index()),
        b1[:, 2 * part : 2 * part + 8, :],
        b2[:, part : part + 8, :],
        b1[:, 2 * part + 8 :, :],
    ]
    count = ring * 2
    for i, block in enumerate(blocks):
        block = block.astype(F32)
        for j in range(2):
            pair = [block[:, 4 * j + 2 * c : 4 * j + 2 * c + 2, :].reshape(count, width) for c in range(CORES)]
            at = (4 * j + i) * count
            mine[at : at + count, :] = jnp.where(core == 0, pair[0], pair[1])
            theirs[at : at + count, :] = jnp.where(core == 0, pair[1], pair[0])


def merge_kernel(state, back, theirs, keep, send):
    line = lax.broadcasted_iota(I32, (8, state.shape[1]), 0)
    scale = 16.0 * math.log2(math.e)
    for i, out in enumerate((keep, send)):
        a, b = state[8 * i : 8 * i + 8, :], back[8 * i : 8 * i + 8, :]
        top = jnp.maximum(a[0:1, :], b[0:1, :])
        total = sum(s[1:2, :] * jnp.exp2((s[0:1, :] - top) * scale) for s in (a, b))
        out[:8, :] = jnp.where(line == 0, top, jnp.where(line == 1, total, a + b))
    send[8:, :] = theirs[...]


def last_kernel(keep, got, mine, bank, loss, next_bank):
    tops = [keep[0:1, :], got[0:1, :]]
    top = jnp.maximum(*tops)
    total = sum(s[1:2, :] * jnp.exp(16.0 * (t - top)) for s, t in zip((keep, got), tops))
    loss[...] = jnp.log(total) + 16.0 * (top - (keep[2:3, :] + got[2:3, :]))

    core, y_lo = core_index(), y_lo_index()
    count = bank.shape[0]
    lines = mine.shape[0] // 2
    ring = lines // (2 * Y_LO)
    line = lax.broadcasted_iota(I32, (lines, count), 0)
    group = line // (2 * ring)
    place = lax.broadcasted_iota(I32, (lines, count), 1).astype(F32)
    keys, rows = [], []
    for source, ref, base in ((core, mine, 0), (1 - core, got, 8)):
        away = jnp.where(source == 0, group, (Y_LO - group) % Y_LO)
        chip = (line // 2 % ring) * Y_LO + (y_lo + Y_LO - away) % Y_LO
        order = chip * 4 + source * 2 + line % 2
        slot = ref[base + lines : base + 2 * lines, :count]
        keys.append(jnp.where(slot == place, order, -1))
        rows.append(ref[base : base + lines, :].astype(BF16))
    winner = jnp.maximum(*[jnp.max(k, axis=0, keepdims=True) for k in keys])
    written = jnp.zeros(bank.shape, F32)
    found = jnp.zeros((count, 128), F32)
    for key, row in zip(keys, rows):
        chosen = jnp.where((key == winner) & (key >= 0), 1.0, 0.0).astype(BF16)
        contract = (((0,), (0,)), ((), ()))
        written += lax.dot_general(chosen, row, contract, preferred_element_type=F32)
        ones = jnp.ones((lines, 128), BF16)
        found += lax.dot_general(chosen, ones, contract, preferred_element_type=F32)
    next_bank[...] = jnp.where(found[:, :1] > 0.5, written, bank[...].astype(F32)).astype(BF16)


def body(queries, w_input, w_output, item_bank, positives, fresh_rows, owners, slots):
    sds = jax.ShapeDtypeStruct
    count = queries.shape[0]
    members = lax.axis_size("dp")
    devices = lax.axis_size("bank")
    chips = devices // CORES
    ring = chips // Y_LO
    part, width = item_bank.shape[0] // 2, item_bank.shape[1]
    half = w_input.shape[1] // CORES
    tall = w_input.shape[0] + w_output.size // CORES // half

    columns = [[z * Y_LO * CORES + i for z in range(ring)] for i in range(Y_LO * CORES)]
    swap = [(i, i ^ 1) for i in range(devices)]

    def around(a, delta):
        pairs = []
        for i in range(devices * members):
            x, up = i % X, i // members % CORES == 0
            pairs.append((i, i - x + (x + (delta if up else -delta)) % X))
        return lax.ppermute(a, ("bank", "dp"), pairs)

    def move_y(a, to):
        return lax.ppermute(a, ("bank", "dp"), along_y(devices, members, to))

    w_mine, box_send = call(
        first_kernel,
        (sds((tall, half), BF16), sds((ring, part + Y_LO * 8, width), BF16)),
        (w_input, w_output, owners.reshape(1, -1), slots.reshape(1, -1), fresh_rows, item_bank),
        [
            VMEM(w_input.shape, BF16),
            VMEM(w_output.shape, BF16),
            VMEM((1, owners.shape[0]), I32),
            VMEM((1, slots.shape[0]), I32),
            VMEM(fresh_rows.shape, BF16),
            VMEM((part, width), BF16),
            VMEM((ring, Y_LO * 8, width), BF16),
            pltpu.SemaphoreType.DMA((7 + ring,)),
        ],
        ins=pl.ANY,
        space=(VMEM, pl.ANY),
        limit=MOST,
    )
    b0 = lax.all_to_all(box_send, "bank", 0, 0, axis_index_groups=columns, tiled=True)
    w_swapped = move_y(w_mine, [[6, 7, 4, 5, 2, 3, 0, 1]] * CORES)
    q_other = lax.ppermute(queries, "bank", swap)
    b2 = call(two_kernel, sds((ring, part + 16, width), BF16), (b0,))
    b2 = move_y(b2, [[y + step for y in range(Y)] for step in (2, -2)])
    b1 = call(one_kernel, sds((ring, 2 * part + 16, width), BF16), (b0, b2))
    b1 = move_y(b1, [[y + step for y in range(Y)] for step in (1, -1)])
    w_both = call(join_kernel, sds((2 * tall, half), BF16), (w_mine, w_swapped), cost=LARGE)
    weights = [w_both] + [around(w_both, delta) for delta in range(1, X)]
    b0, q_other = lax.optimization_barrier((b0, q_other))
    mine = call(
        tower_kernel,
        sds((CORES * count + 8, width), F32),
        (queries, q_other, *weights, positives.reshape(1, -1)),
        [VMEM((w_input.shape[1], half), BF16), VMEM((half, width), BF16)],
    )
    received = lax.ppermute(mine, "bank", swap)
    units = call(unit_kernel, sds((CORES * count + 16, width), BF16), (mine, received))
    partners = lax.ppermute(units, ("bank", "dp"), to_partner(devices, members))

    def score(near, far, units, *refs):
        return call(
            functools.partial(score_kernel, near, far), sds((8 * CORES, count), F32), (units, *refs)
        )

    state = score(True, False, units, b0, b2)
    theirs = score(True, False, partners, b0, b2)
    theirs = score(False, True, partners, theirs, b1)
    back = lax.ppermute(theirs, ("bank", "dp"), to_partner(devices, members))
    state = score(False, True, units, state, b1)
    rows = (sds((4 * chips, width), F32),) * 2
    fresh_mine, fresh_theirs = call(fresh_kernel, rows, (b0, b2, b1))
    keep, send = call(
        merge_kernel,
        (sds((8, count), F32), sds((8 + 4 * chips, width), F32)),
        (state, back, fresh_theirs),
    )
    got = lax.ppermute(send, "bank", swap)
    loss, next_bank = call(
        last_kernel,
        (sds((1, count), F32), sds(item_bank.shape, BF16)),
        (keep, got, fresh_mine, item_bank),
    )
    return loss.reshape(count), next_bank


def solution(mesh):
    return jax.shard_map(
        body,
        mesh=mesh,
        in_specs=(
            P(("bank", "dp"), None),
            P("dp", None),
            P("dp", None),
            P("bank", None),
            P(("bank", "dp")),
            P("bank", None),
            P("bank", None),
            P("bank"),
        ),
        out_specs=(P(("bank", "dp")), P("bank", None)),
        check_vma=False,
    )
```

```python
import functools
import math

import jax
import jax.numpy as jnp
from jax import lax
from jax.experimental import pallas as pl
from jax.experimental.pallas import tpu as pltpu
from jax.sharding import PartitionSpec as P

BF16 = jnp.bfloat16
F32 = jnp.float32
I32 = jnp.int32

CORES = 2
X = 4
Y_LO = 4
Y = 8

VMEM = pltpu.VMEM
LIMIT = 48 * 1024 * 1024
MOST = 60 * 1024 * 1024
SMALL = pl.CostEstimate(flops=1 << 10, bytes_accessed=1 << 10, transcendentals=0)
LARGE = pl.CostEstimate(flops=1 << 36, bytes_accessed=1 << 10, transcendentals=0)


def core_index():
    return lax.rem(lax.axis_index("bank"), CORES)


def y_lo_index():
    return lax.rem(lax.div(lax.axis_index("bank"), CORES), Y_LO)


def half_index():
    return lax.rem(lax.rem(lax.axis_index("dp"), X) + core_index(), 2)


def to_partner(devices, members):
    pairs = []
    for b in range(devices):
        for d in range(members):
            x = d % X
            other = (x + 1 if (x + b) % 2 == 0 else x - 1) % X
            pairs.append((b * members + d, b * members + d - x + other))
    return pairs


def along_y(devices, members, moves):
    pairs = []
    for b in range(devices):
        for d in range(members):
            z, lo, core = b // (Y_LO * CORES), b // CORES % Y_LO, b % CORES
            hi, x = d // X, d % X
            y = moves[core][hi * Y_LO + lo] % Y
            to = ((z * Y_LO + y % Y_LO) * CORES + core) * members + y // Y_LO * X + x
            pairs.append((b * members + d, to))
    return pairs


def call(kernel, outs, args, scratch=(), ins=VMEM, space=None, limit=LIMIT, cost=SMALL):
    space = space or jax.tree.map(lambda _: VMEM, outs)
    return pl.pallas_call(
        kernel,
        out_shape=outs,
        in_specs=[pl.BlockSpec(memory_space=ins)] * len(args),
        out_specs=jax.tree.map(lambda _, s: pl.BlockSpec(memory_space=s), outs, space),
        scratch_shapes=list(scratch),
        cost_estimate=cost,
        compiler_params=pltpu.CompilerParams(vmem_limit_bytes=limit),
    )(*args)


def first_kernel(
    w_input_in, w_output_in, owners_in, slots_in, fresh_in, bank_in,
    half, out, w_input, w_output, owners, slots, fresh, bank, sems,
):
    part = bank.shape[0]
    ring = out.shape[0]
    at = pl.multiple_of(half_index() * part, part)
    loads = [
        pltpu.make_async_copy(a, b, sems.at[i])
        for i, (a, b) in enumerate(
            (
                (bank_in.at[pl.ds(at, part)], bank),
                (owners_in, owners),
                (slots_in, slots),
                (fresh_in, fresh),
                (w_input_in, w_input),
                (w_output_in, w_output),
            )
        )
    ]
    for copy in loads:
        copy.start()
    for copy in loads[1:4]:
        copy.wait()
    count = fresh.shape[0]
    owner = owners[...].astype(F32)
    across = jnp.broadcast_to(owner, (count, count))
    earlier = lax.broadcasted_iota(I32, (count, count), 0) < lax.broadcasted_iota(I32, (count, count), 1)
    same = across == across.T
    placed = jnp.sum(jnp.where(same & earlier, 1.0, 0.0), axis=0, keepdims=True)
    key = (owner * 2.0 + placed).astype(I32)
    row = lax.broadcasted_iota(I32, (ring * Y_LO * 8, count), 0)
    wanted = (row // 8) * 4 + (row % 4)
    chosen = wanted == key
    data = jnp.dot(chosen.astype(BF16), fresh[...], preferred_element_type=F32)
    slot = jnp.sum(jnp.where(chosen, slots[...].astype(F32) + 1.0, 0.0), axis=1, keepdims=True) - 1.0
    kind = lax.broadcasted_iota(I32, data.shape, 0) % 8
    both = jnp.where(kind < 4, data, slot).astype(BF16)
    out[:, part:, :] = both.reshape(ring, Y_LO * 8, both.shape[1])
    loads[0].wait()
    for z in range(ring):
        out[z, :part, :] = bank[...]
    for copy in loads[4:]:
        copy.wait()
    tall, width = w_input.shape
    unit = w_output.shape[0] // CORES
    step = half.shape[0] - tall
    wide = w_output.shape[1]

    def write(core):
        picked = [w_input[:, j + core * unit : j + (core + 1) * unit] for j in range(0, width, CORES * unit)]
        half[:tall, :] = jnp.concatenate(picked, axis=1)
        for i in range(unit // step):
            at = core * unit + i * step
            half[tall:, i * wide : (i + 1) * wide] = w_output[at : at + step, :]

    for core in range(CORES):
        pl.when(core_index() == core)(functools.partial(write, core))


def join_kernel(own, other, out):
    rows = own.shape[0]
    out[:rows, :] = own[...]
    out[rows:, :] = other[...]


def tower_kernel(q_own, q_other, w0, w1, w2, w3, positives, out, first, last):
    d = lax.axis_index("dp")
    x, y_hi = lax.rem(d, X), lax.div(d, X)
    count, depth = q_own.shape
    wide = out.shape[1]
    members = lax.axis_size("dp")
    rows = depth // members
    both = w0.shape[0] // 2
    tall = both - rows
    unit = tall * (w0.shape[1] // wide)
    for delta, w in enumerate((w0, w1, w2, w3)):
        for swapped in range(2):
            hi = jnp.where(swapped == 1, 1 - y_hi, y_hi)
            source = hi * X + lax.rem(x + X - away_of(delta), X)
            base = swapped * both
            first[pl.ds(pl.multiple_of(source * rows, rows), rows), :] = w[base : base + rows, :]
            for i in range(unit // tall):
                at = pl.multiple_of(source * unit + i * tall, tall)
                last[pl.ds(at, tall), :] = w[base + rows : base + both, i * wide : (i + 1) * wide]
    for i, q in enumerate((q_own, q_other)):
        v = jnp.dot(q[...], first[...], preferred_element_type=F32)
        v = (0.5 * v) * (1.0 + jnp.tanh(0.5 * v))
        out[i * count : (i + 1) * count, :] = jnp.dot(
            v.astype(BF16), last[...], preferred_element_type=F32
        )
    out[CORES * count :, :] = jnp.broadcast_to(positives[...].astype(F32), (8, wide))


def away_of(i):
    return jnp.where(core_index() == 0, i, (4 - i) % 4)


def pick(box, part, which):
    rows = [box[:, part + 8 * j : part + 8 * (j + 1), :] for j in range(Y_LO)]
    out = rows[0]
    for j in range(1, Y_LO):
        out = jnp.where(which == j, rows[j], out)
    return out


def two_kernel(box, out):
    y_lo = y_lo_index()
    part = out.shape[1] - 16
    out[:, :part, :] = box[:, :part, :]
    fresh = [pick(box, part, lax.rem(y_lo + away_of(i), Y_LO)) for i in (2, 3)]
    out[:, part:, :] = jnp.concatenate(fresh, axis=1)


def one_kernel(box, two, out):
    part = two.shape[1] - 16
    out[:, :part, :] = box[:, :part, :]
    out[:, part : 2 * part, :] = two[:, :part, :]
    own = pick(box, part, lax.rem(y_lo_index() + away_of(1), Y_LO))
    out[:, 2 * part :, :] = jnp.concatenate([own, two[:, part + 8 :, :]], axis=1)


def unit_kernel(mine, received, out):
    count = (mine.shape[0] - 8) // CORES
    line = lax.broadcasted_iota(I32, (16, mine.shape[1]), 0)
    tail = jnp.zeros(line.shape, F32)
    for i, place in enumerate((mine, received)):
        j = 1 - i
        embedding = mine[i * count : (i + 1) * count, :] + received[j * count : (j + 1) * count, :]
        norm = lax.rsqrt(jnp.sum(embedding * embedding, axis=1, keepdims=True) + 1e-06)
        out[i * count : (i + 1) * count, :] = (embedding * norm).astype(BF16)
        positive = place[CORES * count : CORES * count + 1, :].astype(I32)
        tail = jnp.where(line == 2 * i, (positive // 128).astype(F32), tail)
        tail = jnp.where(line == 2 * i + 1, (positive % 128).astype(F32), tail)
    out[CORES * count :, :] = tail.astype(BF16)


def score_kernel(near, far, units, *refs):
    out = refs[-1]
    old = None if near else refs[0]
    core, y_lo, half = core_index(), y_lo_index(), half_index()
    ring, count = refs[1].shape[0], out.shape[1]
    part = refs[1].shape[1] - 16 if near else (refs[1].shape[1] - 16) // 2
    boxes = []
    if near:
        boxes += [(0, refs[0], 0), (2, refs[1], 0)]
    if far:
        boxes += [(1, refs[-2], 0), (3, refs[-2], part)]
    scale = 16.0 * math.log2(math.e)
    local = ring * part
    number = lax.broadcasted_iota(I32, (local, count), 0)
    line = lax.broadcasted_iota(I32, (8, count), 0)
    tail = units[CORES * count :, :].astype(F32)
    for i in range(CORES):
        unit = units[i * count : (i + 1) * count, :]
        block = tail[2 * i : 2 * i + 1, :].astype(I32)
        row = tail[2 * i + 1 : 2 * i + 2, :].astype(I32)
        chip = block // CORES
        away = (y_lo - chip % Y_LO + Y_LO) % Y_LO
        at = (chip // Y_LO) * part + row % part
        at = jnp.where((block % CORES == core) & (row // part == half), at, -1)
        top = total = picked = None
        if old is not None:
            top, total, picked = (old[8 * i + k : 8 * i + k + 1, :] for k in range(3))
        for delta, box, base in boxes:
            bank = box[:, base : base + part, :].reshape(local, box.shape[2])
            d = lax.dot_general(bank, unit, (((1,), (1,)), ((), ())), preferred_element_type=F32)
            high = jnp.max(d, axis=0, keepdims=True)
            hit = number == jnp.where(away == away_of(delta), at, -1)
            here = jnp.sum(jnp.where(hit, d, 0.0), axis=0, keepdims=True)
            if top is None:
                top, picked = high, here
                total = jnp.sum(jnp.exp2((d - top) * scale), axis=0, keepdims=True)
            else:
                before, top = top, jnp.maximum(top, high)
                total = total * jnp.exp2((before - top) * scale)
                total += jnp.sum(jnp.exp2((d - top) * scale), axis=0, keepdims=True)
                picked += here
        out[8 * i : 8 * i + 8, :] = jnp.where(
            line == 0, top, jnp.where(line == 1, total, jnp.where(line == 2, picked, 0.0))
        )


def fresh_kernel(b0, b2, b1, mine, theirs):
    core = core_index()
    ring, width = b2.shape[0], b2.shape[2]
    part = b2.shape[1] - 16
    blocks = [
        pick(b0, part, y_lo_index()),
        b1[:, 2 * part : 2 * part + 8, :],
        b2[:, part : part + 8, :],
        b1[:, 2 * part + 8 :, :],
    ]
    count = ring * 2
    for i, block in enumerate(blocks):
        block = block.astype(F32)
        for j in range(2):
            pair = [block[:, 4 * j + 2 * c : 4 * j + 2 * c + 2, :].reshape(count, width) for c in range(CORES)]
            at = (4 * j + i) * count
            mine[at : at + count, :] = jnp.where(core == 0, pair[0], pair[1])
            theirs[at : at + count, :] = jnp.where(core == 0, pair[1], pair[0])


def merge_kernel(state, back, theirs, keep, send):
    line = lax.broadcasted_iota(I32, (8, state.shape[1]), 0)
    scale = 16.0 * math.log2(math.e)
    for i, out in enumerate((keep, send)):
        a, b = state[8 * i : 8 * i + 8, :], back[8 * i : 8 * i + 8, :]
        top = jnp.maximum(a[0:1, :], b[0:1, :])
        total = sum(s[1:2, :] * jnp.exp2((s[0:1, :] - top) * scale) for s in (a, b))
        out[:8, :] = jnp.where(line == 0, top, jnp.where(line == 1, total, a + b))
    send[8:, :] = theirs[...]


def last_kernel(keep, got, mine, bank, loss, next_bank):
    tops = [keep[0:1, :], got[0:1, :]]
    top = jnp.maximum(*tops)
    total = sum(s[1:2, :] * jnp.exp(16.0 * (t - top)) for s, t in zip((keep, got), tops))
    loss[...] = jnp.log(total) + 16.0 * (top - (keep[2:3, :] + got[2:3, :]))

    core, y_lo = core_index(), y_lo_index()
    count = bank.shape[0]
    lines = mine.shape[0] // 2
    ring = lines // (2 * Y_LO)
    line = lax.broadcasted_iota(I32, (lines, count), 0)
    group = line // (2 * ring)
    place = lax.broadcasted_iota(I32, (lines, count), 1).astype(F32)
    keys, rows = [], []
    for source, ref, base in ((core, mine, 0), (1 - core, got, 8)):
        away = jnp.where(source == 0, group, (Y_LO - group) % Y_LO)
        chip = (line // 2 % ring) * Y_LO + (y_lo + Y_LO - away) % Y_LO
        order = chip * 4 + source * 2 + line % 2
        slot = ref[base + lines : base + 2 * lines, :count]
        keys.append(jnp.where(slot == place, order, -1))
        rows.append(ref[base : base + lines, :].astype(BF16))
    winner = jnp.maximum(*[jnp.max(k, axis=0, keepdims=True) for k in keys])
    written = jnp.zeros(bank.shape, F32)
    found = jnp.zeros((count, 128), F32)
    for key, row in zip(keys, rows):
        chosen = jnp.where((key == winner) & (key >= 0), 1.0, 0.0).astype(BF16)
        contract = (((0,), (0,)), ((), ()))
        written += lax.dot_general(chosen, row, contract, preferred_element_type=F32)
        ones = jnp.ones((lines, 128), BF16)
        found += lax.dot_general(chosen, ones, contract, preferred_element_type=F32)
    next_bank[...] = jnp.where(found[:, :1] > 0.5, written, bank[...].astype(F32)).astype(BF16)


def body(queries, w_input, w_output, item_bank, positives, fresh_rows, owners, slots):
    sds = jax.ShapeDtypeStruct
    count = queries.shape[0]
    members = lax.axis_size("dp")
    devices = lax.axis_size("bank")
    chips = devices // CORES
    ring = chips // Y_LO
    part, width = item_bank.shape[0] // 2, item_bank.shape[1]
    half = w_input.shape[1] // CORES
    tall = w_input.shape[0] + w_output.size // CORES // half

    columns = [[z * Y_LO * CORES + i for z in range(ring)] for i in range(Y_LO * CORES)]
    swap = [(i, i ^ 1) for i in range(devices)]

    def around(a, delta):
        pairs = []
        for i in range(devices * members):
            x, up = i % X, i // members % CORES == 0
            pairs.append((i, i - x + (x + (delta if up else -delta)) % X))
        return lax.ppermute(a, ("bank", "dp"), pairs)

    def move_y(a, to):
        return lax.ppermute(a, ("bank", "dp"), along_y(devices, members, to))

    w_mine, box_send = call(
        first_kernel,
        (sds((tall, half), BF16), sds((ring, part + Y_LO * 8, width), BF16)),
        (w_input, w_output, owners.reshape(1, -1), slots.reshape(1, -1), fresh_rows, item_bank),
        [
            VMEM(w_input.shape, BF16),
            VMEM(w_output.shape, BF16),
            VMEM((1, owners.shape[0]), I32),
            VMEM((1, slots.shape[0]), I32),
            VMEM(fresh_rows.shape, BF16),
            VMEM((part, width), BF16),
            pltpu.SemaphoreType.DMA((6,)),
        ],
        ins=pl.ANY,
        limit=MOST,
    )
    b0 = lax.all_to_all(box_send, "bank", 0, 0, axis_index_groups=columns, tiled=True)
    w_swapped = move_y(w_mine, [[6, 7, 4, 5, 2, 3, 0, 1]] * CORES)
    q_other = lax.ppermute(queries, "bank", swap)
    b2 = call(two_kernel, sds((ring, part + 16, width), BF16), (b0,))
    b2 = move_y(b2, [[y + step for y in range(Y)] for step in (2, -2)])
    b1 = call(one_kernel, sds((ring, 2 * part + 16, width), BF16), (b0, b2))
    b1 = move_y(b1, [[y + step for y in range(Y)] for step in (1, -1)])
    w_both = call(join_kernel, sds((2 * tall, half), BF16), (w_mine, w_swapped), cost=LARGE)
    weights = [w_both] + [around(w_both, delta) for delta in range(1, X)]
    b0, q_other = lax.optimization_barrier((b0, q_other))
    mine = call(
        tower_kernel,
        sds((CORES * count + 8, width), F32),
        (queries, q_other, *weights, positives.reshape(1, -1)),
        [VMEM((w_input.shape[1], half), BF16), VMEM((half, width), BF16)],
    )
    received = lax.ppermute(mine, "bank", swap)
    units = call(unit_kernel, sds((CORES * count + 16, width), BF16), (mine, received))
    partners = lax.ppermute(units, ("bank", "dp"), to_partner(devices, members))

    def score(near, far, units, *refs):
        return call(
            functools.partial(score_kernel, near, far), sds((8 * CORES, count), F32), (units, *refs)
        )

    state = score(True, False, units, b0, b2)
    theirs = score(True, False, partners, b0, b2)
    theirs = score(False, True, partners, theirs, b1)
    back = lax.ppermute(theirs, ("bank", "dp"), to_partner(devices, members))
    state = score(False, True, units, state, b1)
    rows = (sds((4 * chips, width), F32),) * 2
    fresh_mine, fresh_theirs = call(fresh_kernel, rows, (b0, b2, b1))
    keep, send = call(
        merge_kernel,
        (sds((8, count), F32), sds((8 + 4 * chips, width), F32)),
        (state, back, fresh_theirs),
    )
    got = lax.ppermute(send, "bank", swap)
    loss, next_bank = call(
        last_kernel,
        (sds((1, count), F32), sds(item_bank.shape, BF16)),
        (keep, got, fresh_mine, item_bank),
    )
    return loss.reshape(count), next_bank


def solution(mesh):
    return jax.shard_map(
        body,
        mesh=mesh,
        in_specs=(
            P(("bank", "dp"), None),
            P("dp", None),
            P("dp", None),
            P("bank", None),
            P(("bank", "dp")),
            P("bank", None),
            P("bank", None),
            P("bank"),
        ),
        out_specs=(P(("bank", "dp")), P("bank", None)),
        check_vma=False,
    )
```

```python
import functools
import math

import jax
import jax.numpy as jnp
from jax import lax
from jax.experimental import pallas as pl
from jax.experimental.pallas import tpu as pltpu
from jax.sharding import PartitionSpec as P

BF16 = jnp.bfloat16
F32 = jnp.float32
I32 = jnp.int32

CORES = 2
X = 4
Y_LO = 4
Y = 8

TILE = 8

VMEM = pltpu.VMEM
LIMIT = 48 * 1024 * 1024
MOST = 60 * 1024 * 1024
SMALL = pl.CostEstimate(flops=1 << 10, bytes_accessed=1 << 10, transcendentals=0)
LARGE = pl.CostEstimate(flops=1 << 36, bytes_accessed=1 << 10, transcendentals=0)


def core_index():
    return lax.rem(lax.axis_index("bank"), CORES)


def y_lo_index():
    return lax.rem(lax.div(lax.axis_index("bank"), CORES), Y_LO)


def half_index():
    return lax.rem(lax.rem(lax.axis_index("dp"), X) + core_index(), 2)


def to_partner(devices, members):
    pairs = []
    for b in range(devices):
        for d in range(members):
            x = d % X
            other = (x + 1 if (x + b) % 2 == 0 else x - 1) % X
            pairs.append((b * members + d, b * members + d - x + other))
    return pairs


def along_y(devices, members, moves):
    pairs = []
    for b in range(devices):
        for d in range(members):
            z, lo, core = b // (Y_LO * CORES), b // CORES % Y_LO, b % CORES
            hi, x = d // X, d % X
            y = moves[core][hi * Y_LO + lo] % Y
            to = ((z * Y_LO + y % Y_LO) * CORES + core) * members + y // Y_LO * X + x
            pairs.append((b * members + d, to))
    return pairs


def call(kernel, outs, args, scratch=(), ins=VMEM, space=None, limit=LIMIT, cost=SMALL):
    space = space or jax.tree.map(lambda _: VMEM, outs)
    return pl.pallas_call(
        kernel,
        out_shape=outs,
        in_specs=[pl.BlockSpec(memory_space=ins)] * len(args),
        out_specs=jax.tree.map(lambda _, s: pl.BlockSpec(memory_space=s), outs, space),
        scratch_shapes=list(scratch),
        cost_estimate=cost,
        compiler_params=pltpu.CompilerParams(vmem_limit_bytes=limit),
    )(*args)


def first_kernel(
    w_input_in, w_output_in, owners_in, slots_in, fresh_in, bank_in,
    half, out, w_input, w_output, owners, slots, fresh, bank, sems,
):
    part = bank.shape[0]
    ring = out.shape[0]
    at = pl.multiple_of(half_index() * part, part)
    loads = [
        pltpu.make_async_copy(a, b, sems.at[i])
        for i, (a, b) in enumerate(
            (
                (owners_in, owners),
                (slots_in, slots),
                (fresh_in, fresh),
                (bank_in.at[pl.ds(at, part)], bank),
                (w_input_in, w_input),
                (w_output_in, w_output),
            )
        )
    ]
    for copy in loads:
        copy.start()
    for copy in loads[:3]:
        copy.wait()
    count = fresh.shape[0]
    owner = owners[...].astype(F32)
    across = jnp.broadcast_to(owner, (count, count))
    earlier = lax.broadcasted_iota(I32, (count, count), 0) < lax.broadcasted_iota(I32, (count, count), 1)
    same = across == across.T
    placed = jnp.sum(jnp.where(same & earlier, 1.0, 0.0), axis=0, keepdims=True)
    key = (owner * 2.0 + placed).astype(I32)
    rows = out.shape[1] - part
    line = lax.broadcasted_iota(I32, (ring * rows, count), 0)
    inner = line % rows
    base = (line // rows) * (Y_LO * 4)
    left = base + jnp.where(inner < 16, inner, 2 * (inner - 16))
    chosen = left == key
    data = jnp.dot(chosen.astype(BF16), fresh[...], preferred_element_type=F32)
    after = slots[...].astype(F32) + 1.0
    pair = [
        jnp.sum(jnp.where(hit, after, 0.0), axis=1, keepdims=True) - 1.0
        for hit in (chosen, left + 1 == key)
    ]
    kind = lax.broadcasted_iota(I32, data.shape, 0) % rows
    lane = lax.broadcasted_iota(I32, data.shape, 1)
    slot = jnp.where(lane < data.shape[1] // 2, pair[0], pair[1])
    both = jnp.where(kind < 16, data, slot).astype(BF16)
    out[:, part:, :] = both.reshape(ring, rows, both.shape[1])
    loads[3].wait()
    for z in range(ring):
        out[z, :part, :] = bank[...]
    for copy in loads[4:]:
        copy.wait()
    tall, width = w_input.shape
    unit = w_output.shape[0] // CORES
    step = half.shape[0] - tall
    wide = w_output.shape[1]

    def write(core):
        picked = [w_input[:, j + core * unit : j + (core + 1) * unit] for j in range(0, width, CORES * unit)]
        half[:tall, :] = jnp.concatenate(picked, axis=1)
        for i in range(unit // step):
            at = core * unit + i * step
            half[tall:, i * wide : (i + 1) * wide] = w_output[at : at + step, :]

    for core in range(CORES):
        pl.when(core_index() == core)(functools.partial(write, core))


def join_kernel(own, other, out):
    rows = own.shape[0]
    out[:rows, :] = own[...]
    out[rows:, :] = other[...]


def tower_kernel(q_own, q_other, w0, w1, w2, w3, positives, out, first, last):
    d = lax.axis_index("dp")
    x, y_hi = lax.rem(d, X), lax.div(d, X)
    count, depth = q_own.shape
    wide = out.shape[1]
    members = lax.axis_size("dp")
    rows = depth // members
    both = w0.shape[0] // 2
    tall = both - rows
    unit = tall * (w0.shape[1] // wide)
    for delta, w in enumerate((w0, w1, w2, w3)):
        for swapped in range(2):
            hi = jnp.where(swapped == 1, 1 - y_hi, y_hi)
            source = hi * X + lax.rem(x + X - away_of(delta), X)
            base = swapped * both
            first[pl.ds(pl.multiple_of(source * rows, rows), rows), :] = w[base : base + rows, :]
            for i in range(unit // tall):
                at = pl.multiple_of(source * unit + i * tall, tall)
                last[pl.ds(at, tall), :] = w[base + rows : base + both, i * wide : (i + 1) * wide]
    for i, q in enumerate((q_own, q_other)):
        v = jnp.dot(q[...], first[...], preferred_element_type=F32)
        v = (0.5 * v) * (1.0 + jnp.tanh(0.5 * v))
        out[i * count : (i + 1) * count, :] = jnp.dot(
            v.astype(BF16), last[...], preferred_element_type=F32
        )
    out[CORES * count :, :] = jnp.broadcast_to(positives[...].astype(F32), (8, wide))


def away_of(i):
    return jnp.where(core_index() == 0, i, (4 - i) % 4)


def pick(box, part, which):
    half = box.shape[2] // 2
    rows = [box[:, part + 4 * j : part + 4 * (j + 1), :].astype(F32) for j in range(Y_LO)]
    slots = [box[:, part + 16 + 2 * j : part + 18 + 2 * j, :].astype(F32) for j in range(Y_LO)]
    row, slot = rows[0], slots[0]
    for j in range(1, Y_LO):
        row = jnp.where(which == j, rows[j], row)
        slot = jnp.where(which == j, slots[j], slot)
    wide = [
        jnp.concatenate([slot[:, m : m + 1, side * half : (side + 1) * half]] * 2, axis=2)
        for m in range(2)
        for side in range(2)
    ]
    return jnp.concatenate([row, *wide], axis=1).astype(BF16)


def two_kernel(box, out):
    y_lo = y_lo_index()
    part = out.shape[1] - 16
    out[:, :part, :] = box[:, :part, :]
    fresh = [pick(box, part, lax.rem(y_lo + away_of(i), Y_LO)) for i in (2, 3)]
    out[:, part:, :] = jnp.concatenate(fresh, axis=1)


def one_kernel(box, two, out):
    part = two.shape[1] - 16
    out[:, :part, :] = box[:, :part, :]
    out[:, part : 2 * part, :] = two[:, :part, :]
    own = pick(box, part, lax.rem(y_lo_index() + away_of(1), Y_LO))
    out[:, 2 * part :, :] = jnp.concatenate([own, two[:, part + 8 :, :]], axis=1)


def unit_kernel(mine, received, out):
    count = (mine.shape[0] - 8) // CORES
    line = lax.broadcasted_iota(I32, (16, mine.shape[1]), 0)
    tail = jnp.zeros(line.shape, F32)
    for i, place in enumerate((mine, received)):
        j = 1 - i
        embedding = mine[i * count : (i + 1) * count, :] + received[j * count : (j + 1) * count, :]
        norm = lax.rsqrt(jnp.sum(embedding * embedding, axis=1, keepdims=True) + 1e-06)
        out[i * count : (i + 1) * count, :] = (embedding * norm).astype(BF16)
        positive = place[CORES * count : CORES * count + 1, :].astype(I32)
        tail = jnp.where(line == 2 * i, (positive // 128).astype(F32), tail)
        tail = jnp.where(line == 2 * i + 1, (positive % 128).astype(F32), tail)
    out[CORES * count :, :] = tail.astype(BF16)


def score_kernel(near, far, units, *refs):
    out = refs[-1]
    old = None if near else refs[0]
    core, y_lo, half = core_index(), y_lo_index(), half_index()
    ring, count = refs[1].shape[0], out.shape[1]
    part = refs[1].shape[1] - 16 if near else (refs[1].shape[1] - 16) // 2
    boxes = []
    if near:
        boxes += [(0, refs[0], 0), (2, refs[1], 0)]
    if far:
        boxes += [(1, refs[-2], 0), (3, refs[-2], part)]
    scale = 16.0 * math.log2(math.e)
    local = ring * part
    lane = 8
    line = lax.broadcasted_iota(I32, (lane, count), 0)
    tail = units[CORES * count :, :].astype(F32)
    for i in range(CORES):
        unit = units[i * count : (i + 1) * count, :]
        block = tail[2 * i : 2 * i + 1, :].astype(I32)
        row = tail[2 * i + 1 : 2 * i + 2, :].astype(I32)
        chip = block // CORES
        away = (y_lo - chip % Y_LO + Y_LO) % Y_LO
        at = (chip // Y_LO) * part + row % part
        at = jnp.where((block % CORES == core) & (row // part == half), at, -local)
        high = total = None
        picked = jnp.zeros((lane, count), F32)
        for delta, box, base in boxes:
            bank = box[:, base : base + part, :].reshape(local, box.shape[2])
            d = lax.dot_general(bank, unit, (((1,), (1,)), ((), ())), preferred_element_type=F32)
            d = d.reshape(local // lane, lane, count)
            apart = jnp.where(away == away_of(delta), at, -local) - line
            for first in range(0, local // lane, TILE):
                tile = [d[j] for j in range(first, first + TILE)]
                top = functools.reduce(jnp.maximum, tile)
                if high is not None:
                    top = jnp.maximum(top, high)
                here = sum(jnp.exp2((t - top) * scale) for t in tile)
                total = here if high is None else total * jnp.exp2((high - top) * scale) + here
                high = top
                for j, t in enumerate(tile, first):
                    picked += jnp.where(apart == j * lane, t, 0.0)
        top = jnp.max(high, axis=0, keepdims=True)
        if old is not None:
            top = jnp.maximum(top, old[8 * i : 8 * i + 1, :])
        total = jnp.sum(total * jnp.exp2((high - top) * scale), axis=0, keepdims=True)
        picked = jnp.sum(picked, axis=0, keepdims=True)
        if old is not None:
            before, so_far, found = (old[8 * i + k : 8 * i + k + 1, :] for k in range(3))
            total += so_far * jnp.exp2((before - top) * scale)
            picked += found
        out[8 * i : 8 * i + 8, :] = jnp.where(
            line == 0, top, jnp.where(line == 1, total, jnp.where(line == 2, picked, 0.0))
        )


def fresh_kernel(b0, b2, b1, mine, theirs):
    core = core_index()
    ring, width = b2.shape[0], b2.shape[2]
    part = b2.shape[1] - 16
    blocks = [
        pick(b0, part, y_lo_index()),
        b1[:, 2 * part : 2 * part + 8, :],
        b2[:, part : part + 8, :],
        b1[:, 2 * part + 8 :, :],
    ]
    count = ring * 2
    for i, block in enumerate(blocks):
        block = block.astype(F32)
        for j in range(2):
            pair = [block[:, 4 * j + 2 * c : 4 * j + 2 * c + 2, :].reshape(count, width) for c in range(CORES)]
            at = (4 * j + i) * count
            mine[at : at + count, :] = jnp.where(core == 0, pair[0], pair[1])
            theirs[at : at + count, :] = jnp.where(core == 0, pair[1], pair[0])


def merge_kernel(state, back, theirs, keep, send):
    line = lax.broadcasted_iota(I32, (8, state.shape[1]), 0)
    scale = 16.0 * math.log2(math.e)
    for i, out in enumerate((keep, send)):
        a, b = state[8 * i : 8 * i + 8, :], back[8 * i : 8 * i + 8, :]
        top = jnp.maximum(a[0:1, :], b[0:1, :])
        total = sum(s[1:2, :] * jnp.exp2((s[0:1, :] - top) * scale) for s in (a, b))
        out[:8, :] = jnp.where(line == 0, top, jnp.where(line == 1, total, a + b))
    send[8:, :] = theirs[...]


def last_kernel(keep, got, mine, bank, loss, next_bank):
    tops = [keep[0:1, :], got[0:1, :]]
    top = jnp.maximum(*tops)
    total = sum(s[1:2, :] * jnp.exp(16.0 * (t - top)) for s, t in zip((keep, got), tops))
    loss[...] = jnp.log(total) + 16.0 * (top - (keep[2:3, :] + got[2:3, :]))

    core, y_lo = core_index(), y_lo_index()
    count = bank.shape[0]
    lines = mine.shape[0] // 2
    ring = lines // (2 * Y_LO)
    line = lax.broadcasted_iota(I32, (lines, count), 0)
    group = line // (2 * ring)
    place = lax.broadcasted_iota(I32, (lines, count), 1).astype(F32)
    keys, rows = [], []
    for source, ref, base in ((core, mine, 0), (1 - core, got, 8)):
        away = jnp.where(source == 0, group, (Y_LO - group) % Y_LO)
        chip = (line // 2 % ring) * Y_LO + (y_lo + Y_LO - away) % Y_LO
        order = chip * 4 + source * 2 + line % 2
        slot = ref[base + lines : base + 2 * lines, :count]
        keys.append(jnp.where(slot == place, order, -1))
        rows.append(ref[base : base + lines, :].astype(BF16))
    winner = jnp.maximum(*[jnp.max(k, axis=0, keepdims=True) for k in keys])
    written = jnp.zeros(bank.shape, F32)
    found = jnp.zeros((count, 128), F32)
    for key, row in zip(keys, rows):
        chosen = jnp.where((key == winner) & (key >= 0), 1.0, 0.0).astype(BF16)
        contract = (((0,), (0,)), ((), ()))
        written += lax.dot_general(chosen, row, contract, preferred_element_type=F32)
        ones = jnp.ones((lines, 128), BF16)
        found += lax.dot_general(chosen, ones, contract, preferred_element_type=F32)
    next_bank[...] = jnp.where(found[:, :1] > 0.5, written, bank[...].astype(F32)).astype(BF16)


def body(queries, w_input, w_output, item_bank, positives, fresh_rows, owners, slots):
    sds = jax.ShapeDtypeStruct
    count = queries.shape[0]
    members = lax.axis_size("dp")
    devices = lax.axis_size("bank")
    chips = devices // CORES
    ring = chips // Y_LO
    part, width = item_bank.shape[0] // 2, item_bank.shape[1]
    half = w_input.shape[1] // CORES
    tall = w_input.shape[0] + w_output.size // CORES // half

    columns = [[z * Y_LO * CORES + i for z in range(ring)] for i in range(Y_LO * CORES)]
    swap = [(i, i ^ 1) for i in range(devices)]

    def around(a, delta):
        pairs = []
        for i in range(devices * members):
            x, up = i % X, i // members % CORES == 0
            pairs.append((i, i - x + (x + (delta if up else -delta)) % X))
        return lax.ppermute(a, ("bank", "dp"), pairs)

    def move_y(a, to):
        return lax.ppermute(a, ("bank", "dp"), along_y(devices, members, to))

    w_mine, box_send = call(
        first_kernel,
        (sds((tall, half), BF16), sds((ring, part + Y_LO * 6, width), BF16)),
        (w_input, w_output, owners.reshape(1, -1), slots.reshape(1, -1), fresh_rows, item_bank),
        [
            VMEM(w_input.shape, BF16),
            VMEM(w_output.shape, BF16),
            VMEM((1, owners.shape[0]), I32),
            VMEM((1, slots.shape[0]), I32),
            VMEM(fresh_rows.shape, BF16),
            VMEM((part, width), BF16),
            pltpu.SemaphoreType.DMA((6,)),
        ],
        ins=pl.ANY,
        limit=MOST,
    )
    b0 = lax.all_to_all(box_send, "bank", 0, 0, axis_index_groups=columns, tiled=True)
    w_swapped = move_y(w_mine, [[6, 7, 4, 5, 2, 3, 0, 1]] * CORES)
    q_other = lax.ppermute(queries, "bank", swap)
    b2 = call(two_kernel, sds((ring, part + 16, width), BF16), (b0,))
    b2 = move_y(b2, [[y + step for y in range(Y)] for step in (2, -2)])
    b1 = call(one_kernel, sds((ring, 2 * part + 16, width), BF16), (b0, b2))
    b1 = move_y(b1, [[y + step for y in range(Y)] for step in (1, -1)])
    w_both = call(join_kernel, sds((2 * tall, half), BF16), (w_mine, w_swapped), cost=LARGE)
    weights = [w_both] + [around(w_both, delta) for delta in range(1, X)]
    b0, q_other = lax.optimization_barrier((b0, q_other))
    mine = call(
        tower_kernel,
        sds((CORES * count + 8, width), F32),
        (queries, q_other, *weights, positives.reshape(1, -1)),
        [VMEM((w_input.shape[1], half), BF16), VMEM((half, width), BF16)],
    )
    received = lax.ppermute(mine, "bank", swap)
    units = call(unit_kernel, sds((CORES * count + 16, width), BF16), (mine, received))
    partners = lax.ppermute(units, ("bank", "dp"), to_partner(devices, members))

    def score(near, far, units, *refs):
        return call(
            functools.partial(score_kernel, near, far), sds((8 * CORES, count), F32), (units, *refs)
        )

    state = score(True, False, units, b0, b2)
    theirs = score(True, False, partners, b0, b2)
    theirs = score(False, True, partners, theirs, b1)
    back = lax.ppermute(theirs, ("bank", "dp"), to_partner(devices, members))
    state = score(False, True, units, state, b1)
    rows = (sds((4 * chips, width), F32),) * 2
    fresh_mine, fresh_theirs = call(fresh_kernel, rows, (b0, b2, b1))
    keep, send = call(
        merge_kernel,
        (sds((8, count), F32), sds((8 + 4 * chips, width), F32)),
        (state, back, fresh_theirs),
    )
    got = lax.ppermute(send, "bank", swap)
    loss, next_bank = call(
        last_kernel,
        (sds((1, count), F32), sds(item_bank.shape, BF16)),
        (keep, got, fresh_mine, item_bank),
    )
    return loss.reshape(count), next_bank


def solution(mesh):
    return jax.shard_map(
        body,
        mesh=mesh,
        in_specs=(
            P(("bank", "dp"), None),
            P("dp", None),
            P("dp", None),
            P("bank", None),
            P(("bank", "dp")),
            P("bank", None),
            P("bank", None),
            P("bank"),
        ),
        out_specs=(P(("bank", "dp")), P("bank", None)),
        check_vma=False,
    )
```
